256 devices in a mesh: band: 128 (over y, x, z), lev: 2 (over core).
Axes of the slice: x: 4, y: 4, z: 8, core: 2. Of those that a mesh axis runs over, the one named last changes fastest.
Arguments:
- fourier_in: bfloat16 [1280, 2, 8, 4, 1280], P('band', None, 'lev'), may hold values from -6 to 6
- row_points: int32 [1280], P('band'), may hold values from 20 to 5144, as said below
- gauss_weight: float32 [1280], P('band'), may hold values from 0.5 to 1.5
- pair_order: int32 [640], replicated, may hold values from 0 to 639, each once
- legendre: bfloat16 [640, 1281, 1280], P('band', None, 'lev'), may hold values from -0.25 to 0.25
- diffusion: float32 [8, 2], replicated, may hold values from 0.1 to 10
Outputs:
- fourier_out: bfloat16 [1280, 2, 8, 4, 1280], P('band', None, 'lev')
The draws below stay inside these ranges and needn't reach their ends.
Inputs may be any that keep to these rules, and one draw needn't show every extreme that they name: `row_points`: row i holds 20 + 4 i, 24 + 4 i or 28 + 4 i points; the last row holds 28 + 4 (1279). `pair_order`: every pair index appears once.
All inputs are finite; a program needn't handle non-finite values.
Results may differ from the reference program's by a relative error of at most 0.0063.
Values may be sent and summed in bfloat16 or wider, within the bound.
No kernel may reach another device: no remote copies, remote signals or barrier semaphores. Data moves between devices by JAX's collectives and lax.ppermute only.
A program may use at most 128 MiB of HBM per device.

```python
import math
import jax
import jax.numpy as jnp
from jax import lax

ORDERS = 1280
HLAT = 1280
LEVELS = 8
PAIRS = 640
NROW = 1281


def draw_row_points(key, part):
    key = jax.random.fold_in(key, 5)
    offsets = jax.random.randint(key, (HLAT,), 0, 3)
    offsets = offsets.at[HLAT - 1].set(2)
    return (20 + 4 * jnp.arange(HLAT, dtype=jnp.int32) + 4 * offsets).astype(jnp.int32)


def steps_of(own_key, shape, pieces, least, top_value):
    factor_of, own = 1.0, jax.random.fold_in(own_key, 6)
    for dim, parts in pieces:
        heights = jnp.exp(jax.random.uniform(jax.random.fold_in(own, dim), (parts,), jnp.float32, least / len(pieces), top_value / len(pieces)))
        factor_of = factor_of * jnp.repeat(heights, shape[dim] // parts).reshape([-1 if axis == dim else 1 for axis in range(len(shape))])
    return factor_of


def scatter_about(stream_key, dims, width, reach, split=(), held_as=jnp.bfloat16):
    level = steps_of(stream_key, dims, split, -0.22, 0.18) if split else 1.0
    values = jax.random.normal(stream_key, dims, jnp.float32) * width * level
    return jnp.minimum(jnp.maximum(values, -reach), reach).astype(held_as)


def setup_inputs(seed: int = 0) -> dict:
    streams_of = jax.random.split(jax.random.key(seed), 7)
    return {
        "fourier_in": scatter_about(streams_of[0], (HLAT, 2, LEVELS, 4, ORDERS), 1.0, 6.0, ((0, 128), (2, 2))),
        "row_points": draw_row_points(jax.random.fold_in(streams_of[6], 71), 0),
        "gauss_weight": jnp.clip(0.5 + 1.0 * jax.random.uniform(streams_of[2], (HLAT,), jnp.float32) ** steps_of(streams_of[2], (HLAT,), ((0, 128),), -0.2, 0.2), 0.5, 1.5),
        "pair_order": jax.random.permutation(streams_of[3], PAIRS).astype(jnp.int32),
        "legendre": scatter_about(streams_of[4], (PAIRS, NROW, HLAT), (HLAT // 2) ** -0.5, 0.25, ((0, 128), (2, 2))),
        "diffusion": jnp.clip(jnp.exp(jax.random.uniform(streams_of[5], (LEVELS, 2), jnp.float32, math.log(0.1), math.log(10.0))), 0.1, 10.0),
    }


def make_live(row_points, orders):
    cutoff = jnp.minimum(orders - 1, (row_points - 1) // 2)
    column = lax.broadcasted_iota(jnp.int32, (row_points.shape[0], orders), 1)
    return (column <= cutoff[:, None]).astype(jnp.float32)


def row_layout(first_order, orders):
    midpoint = orders // 2
    row_index = jnp.arange(orders + 1, dtype=jnp.int32)
    odd_block = (row_index > midpoint).astype(jnp.int32)
    position = row_index - odd_block * (midpoint + 1)
    boundary = jnp.where(odd_block[None, :] == 1, ((orders - first_order) // 2)[:, None], ((orders + 1 - first_order) // 2)[:, None])
    leading = position[None, :] < boundary
    second_order = orders - 1 - first_order
    degree = jnp.where(leading, first_order[:, None] + odd_block[None, :] + 2 * position[None, :], second_order[:, None] + odd_block[None, :] + 2 * (position[None, :] - boundary))
    return leading, degree


def reference(fourier_in, row_points, gauss_weight, pair_order, legendre, diffusion):
    orders = ORDERS
    midpoint = orders // 2
    live_cells = make_live(row_points, orders)
    factor = (live_cells * gauss_weight[:, None])[:, None, None, :]
    widened = fourier_in.astype(jnp.float32)
    even_part = ((widened[:, 0] + widened[:, 1]) * factor).astype(jnp.bfloat16)
    odd_part = ((widened[:, 0] - widened[:, 1]) * factor).astype(jnp.bfloat16)
    leading, degree = row_layout(pair_order, orders)
    kappas = jnp.repeat(diffusion, 2, axis=1).reshape(-1)
    levels = fourier_in.shape[2]

    def column_block(source, order_index):
        picked = lax.dynamic_index_in_dim(source, order_index, 3, keepdims=False)
        return picked.reshape(HLAT, levels * 4)

    def per_pair(pair_items):
        pair_table, lead_order, leading_row, degree_row = pair_items
        trail_order = orders - 1 - lead_order
        lower_block = pair_table[: midpoint + 1]
        upper_block = pair_table[midpoint + 1:]
        even_lead = jnp.dot(lower_block, column_block(even_part, lead_order), preferred_element_type=jnp.float32)
        even_trail = jnp.dot(lower_block, column_block(even_part, trail_order), preferred_element_type=jnp.float32)
        odd_lead = jnp.dot(upper_block, column_block(odd_part, lead_order), preferred_element_type=jnp.float32)
        odd_trail = jnp.dot(upper_block, column_block(odd_part, trail_order), preferred_element_type=jnp.float32)
        coeffs = jnp.concatenate([
            jnp.where(leading_row[: midpoint + 1, None], even_lead, even_trail),
            jnp.where(leading_row[midpoint + 1:, None], odd_lead, odd_trail)], axis=0)
        growth = (degree_row * (degree_row + 1)).astype(jnp.float32) / float(orders * (orders + 1))
        damp = 1.0 / (1.0 + growth[:, None] * kappas[None, :])
        spec_pair = (coeffs * damp).astype(jnp.bfloat16)
        zeroes = jnp.zeros_like(spec_pair)
        spec_lead = jnp.where(leading_row[:, None], spec_pair, zeroes)
        spec_trail = jnp.where(leading_row[:, None], zeroes, spec_pair)
        returned = []
        for block_rows, row_range in ((lower_block, slice(0, midpoint + 1)), (upper_block, slice(midpoint + 1, None))):
            for chosen in (spec_lead, spec_trail):
                returned.append(jnp.dot(block_rows.T, chosen[row_range], preferred_element_type=jnp.float32).astype(jnp.bfloat16))
        return jnp.stack(returned)

    returned = lax.map(per_pair, (legendre, pair_order, leading, degree))
    pairs = legendre.shape[0]
    shaped = returned.reshape(pairs, 2, 2, HLAT, levels, 4)
    shaped = jnp.transpose(shaped, (1, 3, 4, 5, 0, 2)).reshape(2, HLAT, levels, 4, orders)
    listing = jnp.stack([pair_order, orders - 1 - pair_order], axis=1).reshape(-1)
    restore = jnp.zeros((orders,), jnp.int32).at[listing].set(jnp.arange(orders, dtype=jnp.int32))
    placed = jnp.take(shaped, restore, axis=4).astype(jnp.float32)
    cell_mask = live_cells[:, None, None, :]
    fourier_out = jnp.stack([(placed[0] + placed[1]) * cell_mask, (placed[0] - placed[1]) * cell_mask], axis=1)
    return fourier_out.astype(jnp.bfloat16)
```

```python
import functools

import jax
import jax.numpy as jnp
from jax import lax
from jax.experimental import pallas as pl
from jax.experimental.pallas import tpu as pltpu
from jax.sharding import PartitionSpec as P

F32 = jnp.float32
BF16 = jnp.bfloat16
LANES = 128
NT = (((1,), (1,)), ((), ()))
NN = (((1,), (0,)), ((), ()))
VMEM = pl.BlockSpec(memory_space=pltpu.VMEM)
SMEM = pl.BlockSpec(memory_space=pltpu.SMEM)
TILES = 5
ROWS = 26


def dot(a, b, dims):
    return lax.dot_general(a, b, dims, preferred_element_type=F32)


def one_hot_rows(listing, slot, q, orders, bands):
    slots = listing.shape[1] // bands
    where_ = lax.broadcasted_iota(jnp.int32, (bands, listing.shape[1]), 1)
    owner = lax.broadcasted_iota(jnp.int32, (bands, listing.shape[1]), 0)
    lead = jnp.sum(jnp.where(where_ == owner * slots + slot, listing, 0), axis=1, keepdims=True)
    order = lead if q == 0 else orders - 1 - lead
    column = lax.broadcasted_iota(jnp.int32, (bands, orders), 1)
    return jnp.where(column == order, 1.0, 0.0).astype(BF16)


def cutoff_of(points, orders):
    return jnp.minimum(orders - 1, lax.shift_right_arithmetic(points - 1, 1))


def pack_kernel(x_ref, points_ref, weight_ref, listing_ref, out_ref, sel_ref, fold, wide):
    rows, _, levels, comps, orders = x_ref.shape
    bands = sel_ref.shape[0] // (2 * TILES)
    vc = levels * comps
    group = 2 * vc
    column = lax.broadcasted_iota(jnp.int32, (comps, orders), 1)
    for i in range(rows):
        live = (column <= cutoff_of(points_ref[i], orders)).astype(F32)
        factor = live * weight_ref[i]
        for v in range(levels):
            north = x_ref[i, 0, v].astype(F32)
            south = x_ref[i, 1, v].astype(F32)
            fold[pl.ds(i * group + v * comps, comps), :] = (north + south) * factor
            fold[pl.ds(i * group + vc + v * comps, comps), :] = (north - south) * factor
    folded = fold[...].astype(BF16)
    gap = jnp.zeros((64, orders), BF16)
    first = jnp.concatenate([folded, gap], axis=0)
    second = jnp.concatenate([gap, folded[256:], folded[:256]], axis=0)
    listing = listing_ref[...]
    for j in range(TILES):
        sel0 = one_hot_rows(listing, j, 0, orders, bands)
        sel1 = one_hot_rows(listing, j, 1, orders, bands)
        sel_ref[pl.ds((2 * j) * bands, bands), :] = sel0
        sel_ref[pl.ds((2 * j + 1) * bands, bands), :] = sel1
        v0 = dot(sel0, first, NT)
        v1 = dot(sel1, second, NT)
        tiles = [v0[:, :128], v0[:, 128:256], v0[:, 256:] + v1[:, :128], v1[:, 128:256], v1[:, 256:]]
        for t in range(TILES):
            wide[pl.ds(TILES * j + t, bands, stride=ROWS), :] = tiles[t]
    wide[pl.ds(ROWS - 1, bands, stride=ROWS), :] = jnp.zeros((bands, LANES), F32)
    out_ref[...] = wide[...].astype(BF16)


def split_tiles(tiles):
    return (
        jnp.concatenate([tiles[0], tiles[1], tiles[2][:64]], axis=0),
        jnp.concatenate([tiles[3], tiles[4], tiles[2][64:]], axis=0),
    )


def join_tiles(first, second):
    return [
        first[:128],
        first[128:256],
        jnp.concatenate([first[256:], second[256:]], axis=0),
        second[:128],
        second[128:256],
    ]


def transform_kernel(got_ref, own_ref, other_ref, place_ref, order_ref, kappa_ref, out_ref, wide, held, spread):
    slots, nrows, half = own_ref.shape
    orders = nrows - 1
    bands = got_ref.shape[0] // ROWS
    per_band = orders // bands
    levels = kappa_ref.shape[0] // 2
    vc = 4 * levels
    four = 4 * vc
    band = lax.axis_index("band")
    lev = lax.axis_index("lev")
    wide[...] = got_ref[...].astype(F32)
    for j in range(slots):
        tiles = [jnp.transpose(wide[pl.ds(TILES * j + t, bands, stride=ROWS), :]) for t in range(TILES)]
        for q, both in enumerate(split_tiles(tiles)):
            for p in range(2):
                for i in range(per_band):
                    piece = both[i * 2 * vc + p * vc : i * 2 * vc + (p + 1) * vc]
                    held[pl.ds(j * four + (2 * p + q) * vc, vc), pl.ds(i * bands, bands)] = piece.astype(BF16)
    spread[...] = dot(held[...], place_ref[...], NN).astype(BF16)

    which = lax.broadcasted_iota(jnp.int32, (vc, 1), 0)
    kappa = jnp.zeros((vc, 1), F32)
    for n in range(2 * levels):
        kappa = jnp.where(lax.shift_right_logical(which, 1) == n, kappa_ref[lev * levels + n // 2, n % 2], kappa)

    def rows_of(start, count, slot):
        first_order = order_ref[band * slots + slot]
        second_order = orders - 1 - first_order
        row = start + lax.broadcasted_iota(jnp.int32, (1, count), 1)
        odd = row > orders // 2
        odd_number = odd.astype(jnp.int32)
        position = row - odd_number * (orders // 2 + 1)
        boundary = jnp.where(
            odd,
            lax.shift_right_arithmetic(orders - first_order, 1),
            lax.shift_right_arithmetic(orders + 1 - first_order, 1),
        )
        leading = position < boundary
        degree = jnp.where(
            leading,
            first_order + odd_number + 2 * position,
            second_order + odd_number + 2 * (position - boundary),
        )
        growth = (degree * (degree + 1)).astype(F32) / float(orders * (orders + 1))
        return odd, leading, 1.0 / (1.0 + kappa * growth)

    def damp(coeffs, start, count, slot):
        odd, leading, factor = rows_of(start, count, slot)
        parts = [coeffs[n * vc : (n + 1) * vc] for n in range(4)]
        picked = jnp.where(odd, jnp.where(leading, parts[2], parts[3]), jnp.where(leading, parts[0], parts[1]))
        spectral = picked * factor
        masks = [
            jnp.logical_and(jnp.logical_not(odd), leading),
            jnp.logical_not(jnp.logical_or(odd, leading)),
            jnp.logical_and(odd, leading),
            jnp.logical_and(odd, jnp.logical_not(leading)),
        ]
        return jnp.concatenate([jnp.where(m, spectral, 0.0) for m in masks], axis=0).astype(BF16)

    for j in range(slots):
        mine = spread[pl.ds(j * four, four), :]
        mine_a, mine_b = mine[:, :half], mine[:, half:]
        coeffs = dot(mine_a, own_ref[j, :orders, :], NT) + dot(mine_b, other_ref[j, :orders, :], NT)
        last_a = own_ref[j, pl.ds(orders, 1), :].astype(F32)
        last_b = other_ref[j, pl.ds(orders, 1), :].astype(F32)
        last = jnp.sum(mine_a.astype(F32) * last_a, axis=1, keepdims=True) + jnp.sum(
            mine_b.astype(F32) * last_b, axis=1, keepdims=True
        )
        chosen = damp(coeffs, 0, orders, j)
        chosen_last = damp(last, orders, 1, j).astype(F32)
        held[pl.ds(j * four, four), pl.ds(0, half)] = (
            dot(chosen, own_ref[j, :orders, :], NN) + chosen_last * last_a
        ).astype(BF16)
        held[pl.ds(j * four, four), pl.ds(half, half)] = (
            dot(chosen, other_ref[j, :orders, :], NN) + chosen_last * last_b
        ).astype(BF16)
    back = dot(held[...], place_ref[...], NT)
    for j in range(slots):
        pair = []
        for q in range(2):
            pieces = []
            for i in range(per_band):
                for p in range(2):
                    start = j * four + (2 * p + q) * vc
                    pieces.append(back[start : start + vc, i * bands : (i + 1) * bands])
            pair.append(jnp.concatenate(pieces, axis=0))
        for t, tile in enumerate(join_tiles(*pair)):
            wide[pl.ds(TILES * j + t, bands, stride=ROWS), :] = jnp.transpose(tile)
    wide[pl.ds(ROWS - 1, bands, stride=ROWS), :] = jnp.zeros((bands, LANES), F32)
    out_ref[...] = wide[...].astype(BF16)


def unpack_kernel(got_ref, points_ref, sel_ref, out_ref, wide, gathered, placed):
    rows, _, levels, comps, orders = out_ref.shape
    bands = got_ref.shape[0] // ROWS
    vc = levels * comps
    wide[...] = got_ref[...].astype(F32)
    for j in range(TILES):
        tiles = [jnp.transpose(wide[pl.ds(TILES * j + t, bands, stride=ROWS), :]) for t in range(TILES)]
        for q, both in enumerate(split_tiles(tiles)):
            gathered[:, pl.ds((2 * j + q) * bands, bands)] = both.astype(BF16)
    placed[...] = dot(gathered[...], sel_ref[...], NN)
    column = lax.broadcasted_iota(jnp.int32, (comps, orders), 1)
    for i in range(rows):
        live = (column <= cutoff_of(points_ref[i], orders)).astype(F32)
        for v in range(levels):
            even = placed[pl.ds(i * 2 * vc + v * comps, comps), :]
            odd = placed[pl.ds(i * 2 * vc + vc + v * comps, comps), :]
            out_ref[i, 0, v] = ((even + odd) * live).astype(BF16)
            out_ref[i, 1, v] = ((even - odd) * live).astype(BF16)


def kernel_params(mib):
    return pltpu.CompilerParams(vmem_limit_bytes=mib * 1024 * 1024)


def exchange(packed, bands):
    shaped = packed.reshape(bands, ROWS // 2, 2, LANES)
    return lax.all_to_all(shaped, "band", split_axis=0, concat_axis=0, tiled=True).reshape(packed.shape)


def on_device(bands, fourier_in, row_points, gauss_weight, pair_order, legendre, diffusion):
    rows, _, levels, comps, orders = fourier_in.shape
    group = 2 * levels * comps * rows
    message = jax.ShapeDtypeStruct((bands * ROWS, LANES), BF16)
    other = lax.ppermute(legendre, "lev", [(0, 1), (1, 0)])
    packed, selector = pl.pallas_call(
        pack_kernel,
        out_shape=(message, jax.ShapeDtypeStruct((orders, orders), BF16)),
        in_specs=[VMEM, SMEM, SMEM, VMEM],
        out_specs=(VMEM, VMEM),
        scratch_shapes=[pltpu.VMEM((group, orders), F32), pltpu.VMEM((bands * ROWS, LANES), F32)],
        compiler_params=kernel_params(32),
        name="pack",
    )(fourier_in, row_points, gauss_weight, pair_order[None, :])
    arrived = exchange(packed, bands)

    lev = lax.axis_index("lev")
    half = orders // 2
    source = lax.broadcasted_iota(jnp.int32, (orders, orders), 0)
    target = lax.broadcasted_iota(jnp.int32, (orders, orders), 1)
    latitude = (source % bands) * rows + source // bands
    turned = jnp.where(latitude >= half, latitude - half, latitude + half)
    place = (jnp.where(lev == 0, latitude, turned) == target).astype(BF16)

    produced = pl.pallas_call(
        transform_kernel,
        out_shape=message,
        in_specs=[VMEM, VMEM, VMEM, VMEM, SMEM, SMEM],
        out_specs=VMEM,
        scratch_shapes=[
            pltpu.VMEM((bands * ROWS, LANES), F32),
            pltpu.VMEM((group, orders), BF16),
            pltpu.VMEM((group, orders), BF16),
        ],
        compiler_params=kernel_params(56),
        name="transform",
    )(arrived, legendre, other, place, pair_order, diffusion)
    landed = exchange(produced, bands)
    return pl.pallas_call(
        unpack_kernel,
        out_shape=jax.ShapeDtypeStruct(fourier_in.shape, BF16),
        in_specs=[VMEM, SMEM, VMEM],
        out_specs=VMEM,
        scratch_shapes=[
            pltpu.VMEM((bands * ROWS, LANES), F32),
            pltpu.VMEM((group, orders), BF16),
            pltpu.VMEM((group, orders), F32),
        ],
        compiler_params=kernel_params(32),
        name="unpack",
    )(landed, row_points, selector)


def solution(mesh):
    in_specs = (
        P("band", None, "lev", None, None),
        P("band"),
        P("band"),
        P(),
        P("band", None, "lev"),
        P(),
    )
    out_specs = P("band", None, "lev", None, None)
    return jax.shard_map(
        functools.partial(on_device, mesh.shape["band"]),
        mesh=mesh,
        in_specs=in_specs,
        out_specs=out_specs,
        check_vma=False,
    )
```

```python
import functools

import jax
import jax.numpy as jnp
from jax import lax
from jax.experimental import pallas as pl
from jax.experimental.pallas import tpu as pltpu
from jax.sharding import PartitionSpec as P

F32 = jnp.float32
BF16 = jnp.bfloat16
LANES = 128
NT = (((1,), (1,)), ((), ()))
NN = (((1,), (0,)), ((), ()))
VMEM = pl.BlockSpec(memory_space=pltpu.VMEM)
ANY = pl.BlockSpec(memory_space=pl.ANY)
SMEM = pl.BlockSpec(memory_space=pltpu.SMEM)
TILES = 5
ROWS = 26


def dot(a, b, dims):
    return lax.dot_general(a, b, dims, preferred_element_type=F32)


def one_hot_rows(listing, slot, q, orders, bands):
    slots = listing.shape[1] // bands
    where_ = lax.broadcasted_iota(jnp.int32, (bands, listing.shape[1]), 1)
    owner = lax.broadcasted_iota(jnp.int32, (bands, listing.shape[1]), 0)
    lead = jnp.sum(jnp.where(where_ == owner * slots + slot, listing, 0), axis=1, keepdims=True)
    order = lead if q == 0 else orders - 1 - lead
    column = lax.broadcasted_iota(jnp.int32, (bands, orders), 1)
    return jnp.where(column == order, 1.0, 0.0).astype(BF16)


def cutoff_of(points, orders):
    return jnp.minimum(orders - 1, lax.shift_right_arithmetic(points - 1, 1))


def pack_kernel(x_ref, points_ref, weight_ref, listing_ref, out_ref, sel_ref, x_held, fold, wide, x_sem):
    rows, _, levels, comps, orders = x_ref.shape
    bands = sel_ref.shape[0] // (2 * TILES)
    vc = levels * comps
    group = 2 * vc
    column = lax.broadcasted_iota(jnp.int32, (comps, orders), 1)
    loads = [pltpu.make_async_copy(x_ref.at[i], x_held.at[i], x_sem.at[i]) for i in range(rows)]
    for load in loads:
        load.start()
    listing = listing_ref[...].reshape(1, orders // 2)
    for q in range(2):
        for j in range(TILES):
            sel_ref[pl.ds((q * TILES + j) * bands, bands), :] = one_hot_rows(listing, j, q, orders, bands)
    for i in range(rows):
        live = (column <= cutoff_of(points_ref[i], orders)).astype(F32)
        factor = live * weight_ref[i]
        loads[i].wait()
        for v in range(levels):
            north = x_held[i, 0, v].astype(F32)
            south = x_held[i, 1, v].astype(F32)
            fold[pl.ds(i * group + v * comps, comps), :] = (north + south) * factor
            fold[pl.ds(i * group + vc + v * comps, comps), :] = (north - south) * factor
    folded = fold[...].astype(BF16)
    gap = jnp.zeros((64, orders), BF16)
    first = jnp.concatenate([folded, gap], axis=0)
    second = jnp.concatenate([gap, folded[256:], folded[:256]], axis=0)
    block = TILES * bands
    v0 = dot(sel_ref[pl.ds(0, block), :], first, NT)
    v1 = dot(sel_ref[pl.ds(block, block), :], second, NT)
    for j in range(TILES):
        a, b = v0[j * bands : (j + 1) * bands], v1[j * bands : (j + 1) * bands]
        tiles = [a[:, :128], a[:, 128:256], a[:, 256:] + b[:, :128], b[:, 128:256], b[:, 256:]]
        for t in range(TILES):
            wide[pl.ds(TILES * j + t, bands, stride=ROWS), :] = tiles[t]
    wide[pl.ds(ROWS - 1, bands, stride=ROWS), :] = jnp.zeros((bands, LANES), F32)
    out_ref[...] = wide[...].astype(BF16)


def split_tiles(tiles):
    return (
        jnp.concatenate([tiles[0], tiles[1], tiles[2][:64]], axis=0),
        jnp.concatenate([tiles[3], tiles[4], tiles[2][64:]], axis=0),
    )


def join_tiles(first, second):
    return [
        first[:128],
        first[128:256],
        jnp.concatenate([first[256:], second[256:]], axis=0),
        second[:128],
        second[128:256],
    ]


def transform_kernel(got_ref, own_ref, other_ref, place_ref, order_ref, kappa_ref, out_ref, wide, held, spread):
    slots, nrows, half = own_ref.shape
    orders = nrows - 1
    bands = got_ref.shape[0] // ROWS
    per_band = orders // bands
    levels = kappa_ref.shape[0] // 2
    vc = 4 * levels
    four = 4 * vc
    band = lax.axis_index("band")
    lev = lax.axis_index("lev")
    wide[...] = got_ref[...].astype(F32)
    for j in range(slots):
        tiles = [jnp.transpose(wide[pl.ds(TILES * j + t, bands, stride=ROWS), :]) for t in range(TILES)]
        for q, both in enumerate(split_tiles(tiles)):
            for p in range(2):
                for i in range(per_band):
                    piece = both[i * 2 * vc + p * vc : i * 2 * vc + (p + 1) * vc]
                    held[pl.ds(j * four + (2 * p + q) * vc, vc), pl.ds(i * bands, bands)] = piece.astype(BF16)
    spread[...] = dot(held[...], place_ref[...], NN).astype(BF16)

    which = lax.broadcasted_iota(jnp.int32, (vc, 1), 0)
    kappa = jnp.zeros((vc, 1), F32)
    for n in range(2 * levels):
        kappa = jnp.where(lax.shift_right_logical(which, 1) == n, kappa_ref[lev * levels + n // 2, n % 2], kappa)

    def rows_of(start, count, slot):
        first_order = order_ref[band * slots + slot]
        second_order = orders - 1 - first_order
        row = start + lax.broadcasted_iota(jnp.int32, (1, count), 1)
        odd = row > orders // 2
        odd_number = odd.astype(jnp.int32)
        position = row - odd_number * (orders // 2 + 1)
        boundary = jnp.where(
            odd,
            lax.shift_right_arithmetic(orders - first_order, 1),
            lax.shift_right_arithmetic(orders + 1 - first_order, 1),
        )
        leading = position < boundary
        degree = jnp.where(
            leading,
            first_order + odd_number + 2 * position,
            second_order + odd_number + 2 * (position - boundary),
        )
        growth = (degree * (degree + 1)).astype(F32) / float(orders * (orders + 1))
        return odd, leading, 1.0 / (1.0 + kappa * growth)

    def damp(coeffs, start, count, slot):
        odd, leading, factor = rows_of(start, count, slot)
        parts = [coeffs[n * vc : (n + 1) * vc] for n in range(4)]
        picked = jnp.where(odd, jnp.where(leading, parts[2], parts[3]), jnp.where(leading, parts[0], parts[1]))
        spectral = picked * factor
        masks = [
            jnp.logical_and(jnp.logical_not(odd), leading),
            jnp.logical_not(jnp.logical_or(odd, leading)),
            jnp.logical_and(odd, leading),
            jnp.logical_and(odd, jnp.logical_not(leading)),
        ]
        return jnp.concatenate([jnp.where(m, spectral, 0.0) for m in masks], axis=0).astype(BF16)

    for j in range(slots):
        mine = spread[pl.ds(j * four, four), :]
        mine_a, mine_b = mine[:, :half], mine[:, half:]
        coeffs = dot(mine_a, own_ref[j, :orders, :], NT) + dot(mine_b, other_ref[j, :orders, :], NT)
        last_a = own_ref[j, pl.ds(orders, 1), :].astype(F32)
        last_b = other_ref[j, pl.ds(orders, 1), :].astype(F32)
        last = jnp.sum(mine_a.astype(F32) * last_a, axis=1, keepdims=True) + jnp.sum(
            mine_b.astype(F32) * last_b, axis=1, keepdims=True
        )
        chosen = damp(coeffs, 0, orders, j)
        chosen_last = damp(last, orders, 1, j).astype(F32)
        held[pl.ds(j * four, four), pl.ds(0, half)] = (
            dot(chosen, own_ref[j, :orders, :], NN) + chosen_last * last_a
        ).astype(BF16)
        held[pl.ds(j * four, four), pl.ds(half, half)] = (
            dot(chosen, other_ref[j, :orders, :], NN) + chosen_last * last_b
        ).astype(BF16)
    back = dot(held[...], place_ref[...], NT)
    for j in range(slots):
        pair = []
        for q in range(2):
            pieces = []
            for i in range(per_band):
                for p in range(2):
                    start = j * four + (2 * p + q) * vc
                    pieces.append(back[start : start + vc, i * bands : (i + 1) * bands])
            pair.append(jnp.concatenate(pieces, axis=0))
        for t, tile in enumerate(join_tiles(*pair)):
            wide[pl.ds(TILES * j + t, bands, stride=ROWS), :] = jnp.transpose(tile)
    wide[pl.ds(ROWS - 1, bands, stride=ROWS), :] = jnp.zeros((bands, LANES), F32)
    out_ref[...] = wide[...].astype(BF16)


def unpack_kernel(got_ref, points_ref, sel_ref, out_ref, wide, gathered, placed):
    rows, _, levels, comps, orders = out_ref.shape
    bands = got_ref.shape[0] // ROWS
    vc = levels * comps
    wide[...] = got_ref[...].astype(F32)
    for j in range(TILES):
        tiles = [jnp.transpose(wide[pl.ds(TILES * j + t, bands, stride=ROWS), :]) for t in range(TILES)]
        for q, both in enumerate(split_tiles(tiles)):
            gathered[:, pl.ds((q * TILES + j) * bands, bands)] = both.astype(BF16)
    placed[...] = dot(gathered[...], sel_ref[...], NN)
    column = lax.broadcasted_iota(jnp.int32, (comps, orders), 1)
    for i in range(rows):
        live = (column <= cutoff_of(points_ref[i], orders)).astype(F32)
        for v in range(levels):
            even = placed[pl.ds(i * 2 * vc + v * comps, comps), :]
            odd = placed[pl.ds(i * 2 * vc + vc + v * comps, comps), :]
            out_ref[i, 0, v] = ((even + odd) * live).astype(BF16)
            out_ref[i, 1, v] = ((even - odd) * live).astype(BF16)


def kernel_params(mib):
    return pltpu.CompilerParams(vmem_limit_bytes=mib * 1024 * 1024)


def exchange(packed, bands):
    shaped = packed.reshape(bands, ROWS // 2, 2, LANES)
    return lax.all_to_all(shaped, "band", split_axis=0, concat_axis=0, tiled=True).reshape(packed.shape)


def on_device(bands, fourier_in, row_points, gauss_weight, pair_order, legendre, diffusion):
    rows, _, levels, comps, orders = fourier_in.shape
    group = 2 * levels * comps * rows
    message = jax.ShapeDtypeStruct((bands * ROWS, LANES), BF16)
    other = lax.ppermute(legendre, "lev", [(0, 1), (1, 0)])
    packed, selector = pl.pallas_call(
        pack_kernel,
        out_shape=(message, jax.ShapeDtypeStruct((orders, orders), BF16)),
        in_specs=[ANY, SMEM, SMEM, VMEM],
        out_specs=(VMEM, VMEM),
        scratch_shapes=[
            pltpu.VMEM(fourier_in.shape, BF16),
            pltpu.VMEM((group, orders), F32),
            pltpu.VMEM((bands * ROWS, LANES), F32),
            pltpu.SemaphoreType.DMA((rows,)),
        ],
        compiler_params=kernel_params(16),
        name="pack",
    )(
        pltpu.with_memory_space_constraint(fourier_in, pltpu.HBM),
        pltpu.with_memory_space_constraint(row_points, pltpu.HBM),
        pltpu.with_memory_space_constraint(gauss_weight, pltpu.HBM),
        pltpu.with_memory_space_constraint(pair_order, pltpu.HBM),
    )
    arrived = exchange(packed, bands)

    lev = lax.axis_index("lev")
    half = orders // 2
    source = lax.broadcasted_iota(jnp.int32, (orders, orders), 0)
    target = lax.broadcasted_iota(jnp.int32, (orders, orders), 1)
    latitude = (source % bands) * rows + source // bands
    turned = jnp.where(latitude >= half, latitude - half, latitude + half)
    place = (jnp.where(lev == 0, latitude, turned) == target).astype(BF16)

    produced = pl.pallas_call(
        transform_kernel,
        out_shape=message,
        in_specs=[VMEM, VMEM, VMEM, VMEM, SMEM, SMEM],
        out_specs=VMEM,
        scratch_shapes=[
            pltpu.VMEM((bands * ROWS, LANES), F32),
            pltpu.VMEM((group, orders), BF16),
            pltpu.VMEM((group, orders), BF16),
        ],
        compiler_params=kernel_params(16),
        name="transform",
    )(
        arrived,
        pltpu.with_memory_space_constraint(legendre, pltpu.VMEM),
        pltpu.with_memory_space_constraint(other, pltpu.VMEM),
        pltpu.with_memory_space_constraint(place, pltpu.VMEM),
        pltpu.with_memory_space_constraint(pair_order, pltpu.HBM),
        pltpu.with_memory_space_constraint(diffusion, pltpu.HBM),
    )
    landed = exchange(produced, bands)
    return pl.pallas_call(
        unpack_kernel,
        out_shape=jax.ShapeDtypeStruct(fourier_in.shape, BF16),
        in_specs=[VMEM, SMEM, VMEM],
        out_specs=VMEM,
        scratch_shapes=[
            pltpu.VMEM((bands * ROWS, LANES), F32),
            pltpu.VMEM((group, orders), BF16),
            pltpu.VMEM((group, orders), F32),
        ],
        compiler_params=kernel_params(16),
        name="unpack",
    )(landed, pltpu.with_memory_space_constraint(row_points, pltpu.HBM), selector)


def solution(mesh):
    in_specs = (
        P("band", None, "lev", None, None),
        P("band"),
        P("band"),
        P(),
        P("band", None, "lev"),
        P(),
    )
    out_specs = P("band", None, "lev", None, None)
    return jax.shard_map(
        functools.partial(on_device, mesh.shape["band"]),
        mesh=mesh,
        in_specs=in_specs,
        out_specs=out_specs,
        check_vma=False,
    )
```

```python
import functools

import jax
import jax.numpy as jnp
from jax import lax
from jax.experimental import pallas as pl
from jax.experimental.pallas import tpu as pltpu
from jax.sharding import PartitionSpec as P

F32 = jnp.float32
BF16 = jnp.bfloat16
LANES = 128
HALF = LANES // 2
NT = (((1,), (1,)), ((), ()))
NN = (((1,), (0,)), ((), ()))
VMEM = pl.BlockSpec(memory_space=pltpu.VMEM)
SMEM = pl.BlockSpec(memory_space=pltpu.SMEM)
ANY = pl.BlockSpec(memory_space=pl.ANY)
TILES = 5
ROWS = 26


def dot(a, b, dims):
    return lax.dot_general(a, b, dims, preferred_element_type=F32)


def one_hot_rows(listing, slot, q, orders, bands):
    slots = listing.shape[1] // bands
    where_ = lax.broadcasted_iota(jnp.int32, (bands, listing.shape[1]), 1)
    owner = lax.broadcasted_iota(jnp.int32, (bands, listing.shape[1]), 0)
    lead = jnp.sum(jnp.where(where_ == owner * slots + slot, listing, 0), axis=1, keepdims=True)
    order = lead if q == 0 else orders - 1 - lead
    column = lax.broadcasted_iota(jnp.int32, (bands, orders), 1)
    return jnp.where(column == order, 1.0, 0.0).astype(BF16)


def cutoff_of(points, orders):
    return jnp.minimum(orders - 1, lax.shift_right_arithmetic(points - 1, 1))


def message_rows(wide, row, bands):
    return wide.at[pl.ds(row, bands, stride=ROWS), :]


def pack_kernel(
    x_ref, points_ref, weight_ref, listing_ref, out_ref, sel_out, x_held, sel_ref, fold, wide, narrow, x_sem, sel_sem, out_sem
):
    rows, _, levels, comps, orders = x_ref.shape
    bands = sel_ref.shape[0] // (2 * TILES)
    vc = levels * comps
    group = 2 * vc
    column = lax.broadcasted_iota(jnp.int32, (comps, orders), 1)
    loads = [pltpu.make_async_copy(x_ref.at[i], x_held.at[i], x_sem.at[i]) for i in range(rows)]
    for load in loads:
        load.start()
    listing = listing_ref[...].reshape(1, orders // 2)
    for j in range(TILES):
        for q in range(2):
            sel_ref[pl.ds((2 * j + q) * bands, bands), :] = one_hot_rows(listing, j, q, orders, bands)
    keep = pltpu.make_async_copy(sel_ref, sel_out, sel_sem)
    keep.start()
    for i in range(rows):
        live = (column <= cutoff_of(points_ref[i], orders)).astype(F32)
        factor = live * weight_ref[i]
        loads[i].wait()
        for v in range(levels):
            north = x_held[i, 0, v].astype(F32)
            south = x_held[i, 1, v].astype(F32)
            fold[pl.ds(i * group + v * comps, comps), :] = (north + south) * factor
            fold[pl.ds(i * group + vc + v * comps, comps), :] = (north - south) * factor
    folded = fold[...].astype(BF16)
    per_tile = LANES // group
    for tile in range(3):
        first = tile * per_tile
        count = min(per_tile, 2 * TILES - first)
        sent = dot(folded, sel_ref[pl.ds(first * bands, count * bands), :], NT)

        def block(i):
            return [sent[i * group : (i + 1) * group, n * bands : (n + 1) * bands] for n in range(count)]

        for pair in range(rows // 2):
            if tile == 2:
                both = jnp.concatenate(block(2 * pair) + block(2 * pair + 1), axis=0)
                message_rows(wide, TILES * pair + 2, bands)[...] = jnp.transpose(both)
            else:
                for odd in range(2):
                    one = jnp.concatenate(block(2 * pair + odd), axis=0)
                    message_rows(wide, TILES * pair + 3 * odd + tile, bands)[...] = jnp.transpose(one)
    message_rows(wide, ROWS - 1, bands)[...] = jnp.zeros((bands, LANES), F32)
    send_out(wide, narrow, out_ref, out_sem)
    keep.wait()


def send_out(wide, narrow, out_ref, sem):
    parts = sem.shape[0]
    size = narrow.shape[0] // parts
    stores = []
    for n in range(parts):
        piece = pl.ds(n * size, size)
        narrow[piece, :] = wide[piece, :].astype(BF16)
        stores.append(pltpu.make_async_copy(narrow.at[piece], out_ref.at[piece], sem.at[n]))
        stores[-1].start()
    for store in stores:
        store.wait()


def gain_kernel(order_ref, kappa_ref, gain_ref):
    slots = gain_ref.shape[0]
    orders = gain_ref.shape[2] - LANES
    levels = kappa_ref.shape[0] // 2
    vc = 4 * levels
    band = lax.axis_index("band")
    lev = lax.axis_index("lev")
    which = lax.broadcasted_iota(jnp.int32, (vc, 1), 0)
    kappa = jnp.zeros((vc, 1), F32)
    for n in range(2 * levels):
        kappa = jnp.where(lax.shift_right_logical(which, 1) == n, kappa_ref[lev * levels + n // 2, n % 2], kappa)
    row = lax.broadcasted_iota(jnp.int32, (1, gain_ref.shape[2]), 1)
    odd = row > orders // 2
    odd_number = odd.astype(jnp.int32)
    position = row - odd_number * (orders // 2 + 1)
    for j in range(slots):
        first_order = order_ref[band * slots + j]
        second_order = orders - 1 - first_order
        boundary = jnp.where(
            odd,
            lax.shift_right_arithmetic(orders - first_order, 1),
            lax.shift_right_arithmetic(orders + 1 - first_order, 1),
        )
        leading = position < boundary
        degree = jnp.where(
            leading,
            first_order + odd_number + 2 * position,
            second_order + odd_number + 2 * (position - boundary),
        )
        growth = (degree * (degree + 1)).astype(F32) / float(orders * (orders + 1))
        factor = 1.0 / (1.0 + kappa * growth)
        for q in range(2):
            for p in range(2):
                mask = jnp.logical_and(
                    leading if q == 0 else jnp.logical_not(leading), odd if p == 1 else jnp.logical_not(odd)
                )
                gain_ref[j, pl.ds((2 * q + p) * vc, vc), :] = jnp.where(mask, factor, 0.0)


def transform_kernel(
    got_ref, own_ref, other_ref, gain_ref, out_ref, wide, narrow, grid, back, own_held, other_held, own_sem, other_sem, out_sem
):
    slots, nrows, half = own_held.shape
    orders = nrows - 1
    bands = got_ref.shape[0] // ROWS
    rows = orders // bands
    four = gain_ref.shape[1]
    lev = lax.axis_index("lev")
    own_first = pl.multiple_of(lev * half, LANES)
    other_first = pl.multiple_of((1 - lev) * half, LANES)
    loads = []
    for j in range(slots):
        loads.append(
            (
                pltpu.make_async_copy(own_ref.at[j], own_held.at[j], own_sem.at[j]),
                pltpu.make_async_copy(other_ref.at[j], other_held.at[j], other_sem.at[j]),
            )
        )
        for load in loads[j]:
            load.start()

    def latitude(i, tile):
        return grid.at[pl.ds(tile * orders + i, bands, stride=rows), :]

    wide[...] = got_ref[...].astype(F32)
    for pair in range(rows // 2):
        parts = [message_rows(wide, TILES * pair + u, bands)[...] for u in range(TILES)]
        for tile, part in enumerate(parts[:3]):
            latitude(2 * pair, tile)[...] = part
        for tile, part in enumerate([parts[3], parts[4], pltpu.roll(parts[2], HALF, 1)]):
            latitude(2 * pair + 1, tile)[...] = part

    left = lax.broadcasted_iota(jnp.int32, (orders, LANES), 1) < HALF
    for tile in range(3):
        inside = range(2 * tile, min(2 * tile + 2, slots))
        mine_own = grid[pl.ds(tile * orders + own_first, half), :].astype(BF16)
        mine_other = grid[pl.ds(tile * orders + other_first, half), :].astype(BF16)
        coeffs, last, last_rows = [], [], []
        for j in inside:
            for load in loads[j]:
                load.wait()
            coeffs.append(dot(own_held[j, :orders, :], mine_own, NN) + dot(other_held[j, :orders, :], mine_other, NN))
            row_own, row_other = own_held[j, pl.ds(orders, 1), :], other_held[j, pl.ds(orders, 1), :]
            last.append(dot(row_own, mine_own, NN) + dot(row_other, mine_other, NN))
            last_rows.append((row_own.astype(F32), row_other.astype(F32)))
        both = jnp.where(left, coeffs[0], coeffs[1]) if len(coeffs) > 1 else coeffs[0]
        turned = jnp.transpose(both)
        ends = jnp.transpose(jnp.concatenate(last + [jnp.zeros((8 - len(last), LANES), F32)], axis=0))
        for n, j in enumerate(inside):
            mine = slice(n * four, (n + 1) * four)
            chosen = (turned[mine] * gain_ref[j, :, pl.ds(0, orders)]).astype(BF16)
            chosen_last = (ends[mine, n : n + 1] * gain_ref[j, :, pl.ds(orders, 1)]).astype(BF16).astype(F32)
            lines = pl.ds(j * four, four)
            back[lines, pl.ds(own_first, half)] = (
                dot(chosen, own_held[j, :orders, :], NN) + chosen_last * last_rows[n][0]
            )
            back[lines, pl.ds(other_first, half)] = (
                dot(chosen, other_held[j, :orders, :], NN) + chosen_last * last_rows[n][1]
            )
        grid[pl.ds(tile * orders, orders), :] = jnp.transpose(back[pl.ds(tile * LANES, LANES), :])

    left = lax.broadcasted_iota(jnp.int32, (bands, LANES), 1) < HALF
    for pair in range(rows // 2):
        even = [latitude(2 * pair, tile)[...] for tile in range(3)]
        odd = [latitude(2 * pair + 1, tile)[...] for tile in range(3)]
        parts = [even[0], even[1], jnp.where(left, even[2], pltpu.roll(odd[2], HALF, 1)), odd[0], odd[1]]
        for u, part in enumerate(parts):
            message_rows(wide, TILES * pair + u, bands)[...] = part
    message_rows(wide, ROWS - 1, bands)[...] = jnp.zeros((bands, LANES), F32)
    send_out(wide, narrow, out_ref, out_sem)


def unpack_kernel(got_ref, points_ref, sel_ref, out_ref, wide, gathered, placed):
    rows, _, levels, comps, orders = out_ref.shape
    bands = got_ref.shape[0] // ROWS
    vc = levels * comps
    group = 2 * vc
    per_tile = LANES // group
    wide[...] = got_ref[...].astype(F32)
    for pair in range(rows // 2):
        parts = [jnp.transpose(message_rows(wide, TILES * pair + u, bands)[...]).astype(BF16) for u in range(TILES)]
        for odd in range(2):
            tiles = [parts[3 * odd], parts[3 * odd + 1], parts[2][odd * HALF : (odd + 1) * HALF]]
            for n in range(2 * TILES):
                at = (n % per_tile) * group
                gathered[pl.ds((2 * pair + odd) * group, group), pl.ds(n * bands, bands)] = tiles[n // per_tile][
                    at : at + group
                ]
    placed[...] = dot(gathered[...], sel_ref[...], NN)
    column = lax.broadcasted_iota(jnp.int32, (comps, orders), 1)
    for i in range(rows):
        live = (column <= cutoff_of(points_ref[i], orders)).astype(F32)
        for v in range(levels):
            even = placed[pl.ds(i * group + v * comps, comps), :]
            odd = placed[pl.ds(i * group + vc + v * comps, comps), :]
            out_ref[i, 0, v] = ((even + odd) * live).astype(BF16)
            out_ref[i, 1, v] = ((even - odd) * live).astype(BF16)


def kernel_params(mib):
    return pltpu.CompilerParams(vmem_limit_bytes=mib * 1024 * 1024)


def exchange(packed, bands):
    shaped = packed.reshape(bands, ROWS // 2, 2, LANES)
    return lax.all_to_all(shaped, "band", split_axis=0, concat_axis=0, tiled=True).reshape(packed.shape)


def in_hbm(*arrays):
    return [pltpu.with_memory_space_constraint(a, pltpu.HBM) for a in arrays]


def in_vmem(*arrays):
    return [pltpu.with_memory_space_constraint(a, pltpu.VMEM) for a in arrays]


def on_device(bands, fourier_in, row_points, gauss_weight, pair_order, legendre, diffusion):
    rows, _, levels, comps, orders = fourier_in.shape
    slots, nrows, half = legendre.shape
    group = 2 * levels * comps
    size = (bands * ROWS, LANES)
    message = pltpu.HBM(size, BF16)
    other = lax.ppermute(legendre, "lev", [(0, 1), (1, 0)])
    points, weights, listing, kappas = in_hbm(row_points, gauss_weight, pair_order, diffusion)
    packed, selector = pl.pallas_call(
        pack_kernel,
        out_shape=(message, pltpu.HBM((orders, orders), BF16)),
        in_specs=[ANY, SMEM, SMEM, VMEM],
        out_specs=(ANY, ANY),
        scratch_shapes=[
            pltpu.VMEM(fourier_in.shape, BF16),
            pltpu.VMEM((orders, orders), BF16),
            pltpu.VMEM((group * rows, orders), F32),
            pltpu.VMEM(size, F32),
            pltpu.VMEM(size, BF16),
            pltpu.SemaphoreType.DMA((rows,)),
            pltpu.SemaphoreType.DMA(()),
            pltpu.SemaphoreType.DMA((4,)),
        ],
        compiler_params=kernel_params(16),
        name="pack",
    )(*in_hbm(fourier_in), points, weights, listing)
    arrived = exchange(packed, bands)

    gain = pl.pallas_call(
        gain_kernel,
        out_shape=jax.ShapeDtypeStruct((slots, 2 * group, orders + LANES), F32),
        in_specs=[SMEM, SMEM],
        out_specs=VMEM,
        compiler_params=kernel_params(8),
        name="gain",
    )(listing, kappas)

    produced = pl.pallas_call(
        transform_kernel,
        out_shape=message,
        in_specs=[VMEM, ANY, ANY, VMEM],
        out_specs=ANY,
        scratch_shapes=[
            pltpu.VMEM(size, F32),
            pltpu.VMEM(size, BF16),
            pltpu.VMEM((3 * orders, LANES), F32),
            pltpu.VMEM((3 * LANES, orders), F32),
            pltpu.VMEM(legendre.shape, BF16),
            pltpu.VMEM(legendre.shape, BF16),
            pltpu.SemaphoreType.DMA((slots,)),
            pltpu.SemaphoreType.DMA((slots,)),
            pltpu.SemaphoreType.DMA((4,)),
        ],
        compiler_params=kernel_params(40),
        name="transform",
    )(arrived, *in_hbm(legendre, other), gain)
    landed = exchange(produced, bands)
    return pl.pallas_call(
        unpack_kernel,
        out_shape=jax.ShapeDtypeStruct(fourier_in.shape, BF16),
        in_specs=[VMEM, SMEM, VMEM],
        out_specs=VMEM,
        scratch_shapes=[
            pltpu.VMEM(size, F32),
            pltpu.VMEM((group * rows, orders), BF16),
            pltpu.VMEM((group * rows, orders), F32),
        ],
        compiler_params=kernel_params(16),
        name="unpack",
    )(landed, points, *in_vmem(selector))


def solution(mesh):
    in_specs = (
        P("band", None, "lev", None, None),
        P("band"),
        P("band"),
        P(),
        P("band", None, "lev"),
        P(),
    )
    out_specs = P("band", None, "lev", None, None)
    return jax.shard_map(
        functools.partial(on_device, mesh.shape["band"]),
        mesh=mesh,
        in_specs=in_specs,
        out_specs=out_specs,
        check_vma=False,
    )
```

```python
import functools

import jax
import jax.numpy as jnp
from jax import lax
from jax.experimental import pallas as pl
from jax.experimental.pallas import tpu as pltpu
from jax.sharding import PartitionSpec as P

F32 = jnp.float32
BF16 = jnp.bfloat16
LANES = 128
HALF = LANES // 2
NT = (((1,), (1,)), ((), ()))
NN = (((1,), (0,)), ((), ()))
VMEM = pl.BlockSpec(memory_space=pltpu.VMEM)
SMEM = pl.BlockSpec(memory_space=pltpu.SMEM)
ANY = pl.BlockSpec(memory_space=pl.ANY)
TILES = 5
ROWS = 26


def dot(a, b, dims):
    return lax.dot_general(a, b, dims, preferred_element_type=F32)


def one_hot_rows(listing, slot, q, orders, bands):
    slots = listing.shape[1] // bands
    where_ = lax.broadcasted_iota(jnp.int32, (bands, listing.shape[1]), 1)
    owner = lax.broadcasted_iota(jnp.int32, (bands, listing.shape[1]), 0)
    lead = jnp.sum(jnp.where(where_ == owner * slots + slot, listing, 0), axis=1, keepdims=True)
    order = lead if q == 0 else orders - 1 - lead
    column = lax.broadcasted_iota(jnp.int32, (bands, orders), 1)
    return jnp.where(column == order, 1.0, 0.0).astype(BF16)


def cutoff_of(points, orders):
    return jnp.minimum(orders - 1, lax.shift_right_arithmetic(points - 1, 1))


def message_rows(wide, row, bands):
    return wide.at[pl.ds(row, bands, stride=ROWS), :]


def one_hot(listing_ref, sel_ref):
    orders = sel_ref.shape[1]
    bands = orders // (2 * TILES)
    listing = listing_ref[...].reshape(1, orders // 2)
    for j in range(TILES):
        for q in range(2):
            sel_ref[pl.ds((2 * j + q) * bands, bands), :] = one_hot_rows(listing, j, q, orders, bands)


def pack_kernel(x_ref, points_ref, weight_ref, listing_ref, out_ref, x_held, sel_ref, fold, wide, narrow, x_sem, out_sem):
    rows, _, levels, comps, orders = x_ref.shape
    bands = sel_ref.shape[0] // (2 * TILES)
    vc = levels * comps
    group = 2 * vc
    column = lax.broadcasted_iota(jnp.int32, (comps, orders), 1)
    loads = [pltpu.make_async_copy(x_ref.at[i], x_held.at[i], x_sem.at[i]) for i in range(rows)]
    for load in loads:
        load.start()
    one_hot(listing_ref, sel_ref)
    for i in range(rows):
        live = (column <= cutoff_of(points_ref[i], orders)).astype(F32)
        factor = live * weight_ref[i]
        loads[i].wait()
        for v in range(levels):
            north = x_held[i, 0, v].astype(F32)
            south = x_held[i, 1, v].astype(F32)
            fold[pl.ds(i * group + v * comps, comps), :] = (north + south) * factor
            fold[pl.ds(i * group + vc + v * comps, comps), :] = (north - south) * factor
    folded = fold[...].astype(BF16)
    per_tile = LANES // group
    for tile in range(3):
        first = tile * per_tile
        count = min(per_tile, 2 * TILES - first)
        sent = dot(folded, sel_ref[pl.ds(first * bands, count * bands), :], NT)

        def block(i):
            return [sent[i * group : (i + 1) * group, n * bands : (n + 1) * bands] for n in range(count)]

        for pair in range(rows // 2):
            if tile == 2:
                both = jnp.concatenate(block(2 * pair) + block(2 * pair + 1), axis=0)
                message_rows(wide, TILES * pair + 2, bands)[...] = jnp.transpose(both)
            else:
                for odd in range(2):
                    one = jnp.concatenate(block(2 * pair + odd), axis=0)
                    message_rows(wide, TILES * pair + 3 * odd + tile, bands)[...] = jnp.transpose(one)
    message_rows(wide, ROWS - 1, bands)[...] = jnp.zeros((bands, LANES), F32)
    send_out(wide, narrow, out_ref, out_sem)


def send_out(wide, narrow, out_ref, sem):
    parts = sem.shape[0]
    size = narrow.shape[0] // parts
    stores = []
    for n in range(parts):
        piece = pl.ds(n * size, size)
        narrow[piece, :] = wide[piece, :].astype(BF16)
        stores.append(pltpu.make_async_copy(narrow.at[piece], out_ref.at[piece], sem.at[n]))
        stores[-1].start()
    for store in stores:
        store.wait()


def between_kernel(order_ref, kappa_ref, listing_ref, gain_ref, sel_out, sel_ref, sel_sem):
    one_hot(listing_ref, sel_ref)
    keep = pltpu.make_async_copy(sel_ref, sel_out, sel_sem)
    keep.start()
    slots = gain_ref.shape[0]
    orders = gain_ref.shape[2] - LANES
    levels = kappa_ref.shape[1] // 2
    vc = 4 * levels
    band = lax.axis_index("band")
    lev = lax.axis_index("lev")
    which = lax.broadcasted_iota(jnp.int32, (vc, 1), 0)
    kappa = jnp.zeros((vc, 1), F32)
    for n in range(2 * levels):
        kappa = jnp.where(lax.shift_right_logical(which, 1) == n, kappa_ref[n % 2, lev * levels + n // 2], kappa)
    row = lax.broadcasted_iota(jnp.int32, (1, gain_ref.shape[2]), 1)
    odd = row > orders // 2
    odd_number = odd.astype(jnp.int32)
    position = row - odd_number * (orders // 2 + 1)
    for j in range(slots):
        first_order = order_ref[band * slots + j]
        second_order = orders - 1 - first_order
        boundary = jnp.where(
            odd,
            lax.shift_right_arithmetic(orders - first_order, 1),
            lax.shift_right_arithmetic(orders + 1 - first_order, 1),
        )
        leading = position < boundary
        degree = jnp.where(
            leading,
            first_order + odd_number + 2 * position,
            second_order + odd_number + 2 * (position - boundary),
        )
        growth = (degree * (degree + 1)).astype(F32) / float(orders * (orders + 1))
        factor = 1.0 / (1.0 + kappa * growth)
        for q in range(2):
            for p in range(2):
                mask = jnp.logical_and(
                    leading if q == 0 else jnp.logical_not(leading), odd if p == 1 else jnp.logical_not(odd)
                )
                gain_ref[j, pl.ds((2 * q + p) * vc, vc), :] = jnp.where(mask, factor, 0.0)
    keep.wait()


def transform_kernel(
    got_ref, own_ref, other_ref, gain_ref, out_ref, wide, grid, back, own_held, other_held, own_sem, other_sem
):
    slots, nrows, half = own_held.shape
    orders = nrows - 1
    bands = got_ref.shape[0] // ROWS
    rows = orders // bands
    four = gain_ref.shape[1]
    lev = lax.axis_index("lev")
    own_first = pl.multiple_of(lev * half, LANES)
    other_first = pl.multiple_of((1 - lev) * half, LANES)
    middle = orders // 2
    pieces = [pl.ds(0, middle), pl.ds(middle, nrows - middle)]
    loads = {}
    for j in [slots - 1] + list(range(slots - 1)):
        loads[j] = []
        for n, piece in enumerate(pieces):
            own_load = pltpu.make_async_copy(own_ref.at[j, piece], own_held.at[j, piece], own_sem.at[j, n])
            other_load = pltpu.make_async_copy(other_ref.at[j, piece], other_held.at[j, piece], other_sem.at[j, n])
            loads[j].append((own_load, other_load))

    def start(j):
        for both in loads[j]:
            for load in both:
                load.start()

    start(4)

    def latitude(i, tile):
        return grid.at[pl.ds(tile * orders + i, bands, stride=rows), :]

    wide[...] = got_ref[...].astype(F32)
    right = lax.broadcasted_iota(jnp.int32, (bands, LANES), 1) >= HALF
    second = lax.broadcasted_iota(jnp.int32, (orders, LANES), 1) >= HALF
    columns, coeffs, ends, chosen, chosen_last = {}, {}, {}, {}, {}

    def arrange(tile):
        for pair in range(rows // 2):
            for odd in range(2):
                part = message_rows(wide, TILES * pair + (2 if tile == 2 else 3 * odd + tile), bands)[...]
                latitude(2 * pair + odd, tile)[...] = pltpu.roll(part, HALF, 1) if tile == 2 and odd else part
        columns[tile] = [
            grid[pl.ds(tile * orders + first, half), :].astype(BF16) for first in (own_first, other_first)
        ]

    def forward(j):
        own, other = columns[j // 2]
        parts = []
        for n in range(2):
            for load in loads[j][n]:
                load.wait()
            piece = pl.ds(n * middle, middle)
            parts.append(dot(own_held[j, piece, :], own, NN) + dot(other_held[j, piece, :], other, NN))
        coeffs[j] = jnp.concatenate(parts, axis=0)
        ends[j] = dot(own_held[j, pl.ds(orders, 1), :], own, NN) + dot(other_held[j, pl.ds(orders, 1), :], other, NN)

    def settle(tile):
        inside = [j for j in (2 * tile, 2 * tile + 1) if j < slots]
        both = coeffs[inside[0]] if len(inside) == 1 else jnp.where(second, coeffs[inside[1]], coeffs[inside[0]])
        turned = jnp.transpose(both)
        rest = jnp.zeros((8 - len(inside), LANES), F32)
        turned_ends = jnp.transpose(jnp.concatenate([ends[j] for j in inside] + [rest], axis=0))
        for n, j in enumerate(inside):
            mine = slice(n * four, (n + 1) * four)
            chosen[j] = (turned[mine] * gain_ref[j, :, pl.ds(0, orders)]).astype(BF16)
            chosen_last[j] = (turned_ends[mine, n : n + 1] * gain_ref[j, :, pl.ds(orders, 1)]).astype(BF16).astype(F32)

    def inverse(j):
        for held, first in ((own_held, own_first), (other_held, other_first)):
            back[pl.ds(j * four, four), pl.ds(first, half)] = dot(chosen[j], held[j, :orders, :], NN) + chosen_last[
                j
            ] * held[j, pl.ds(orders, 1), :].astype(F32)

    def finish(tile):
        grid[pl.ds(tile * orders, orders), :] = jnp.transpose(back[pl.ds(tile * LANES, LANES), :])
        for pair in range(rows // 2):
            even, odd = latitude(2 * pair, tile)[...], latitude(2 * pair + 1, tile)[...]
            if tile == 2:
                both = jnp.where(right, pltpu.roll(odd, HALF, 1), even)
                message_rows(wide, TILES * pair + 2, bands)[...] = both
            else:
                message_rows(wide, TILES * pair + tile, bands)[...] = even
                message_rows(wide, TILES * pair + 3 + tile, bands)[...] = odd

    arrange(2)
    start(0)
    arrange(0)
    forward(4)
    start(1)
    forward(0)
    start(2)
    settle(2)
    inverse(4)
    forward(1)
    start(3)
    arrange(1)
    finish(2)
    forward(2)
    settle(0)
    inverse(0)
    forward(3)
    inverse(1)
    finish(0)
    settle(1)
    inverse(2)
    inverse(3)
    finish(1)
    message_rows(wide, ROWS - 1, bands)[...] = jnp.zeros((bands, LANES), F32)
    out_ref[...] = wide[...].astype(BF16)


def unpack_kernel(got_ref, points_ref, sel_ref, out_ref, wide, gathered, placed, held, out_sem):
    rows, _, levels, comps, orders = out_ref.shape
    bands = got_ref.shape[0] // ROWS
    vc = levels * comps
    group = 2 * vc
    per_tile = LANES // group
    wide[...] = got_ref[...].astype(F32)
    for pair in range(rows // 2):
        parts = [jnp.transpose(message_rows(wide, TILES * pair + u, bands)[...]).astype(BF16) for u in range(TILES)]
        for odd in range(2):
            tiles = [parts[3 * odd], parts[3 * odd + 1], parts[2][odd * HALF : (odd + 1) * HALF]]
            for n in range(2 * TILES):
                at = (n % per_tile) * group
                gathered[pl.ds((2 * pair + odd) * group, group), pl.ds(n * bands, bands)] = tiles[n // per_tile][
                    at : at + group
                ]
    width = 2 * LANES
    stores = []
    for n in range(orders // width):
        block = pl.ds(n * width, width)
        placed[:, block] = dot(gathered[...], sel_ref[:, block], NN)
        column = n * width + lax.broadcasted_iota(jnp.int32, (comps, width), 1)
        for i in range(rows):
            live = (column <= cutoff_of(points_ref[i], orders)).astype(F32)
            for v in range(levels):
                even = placed[pl.ds(i * group + v * comps, comps), block]
                odd = placed[pl.ds(i * group + vc + v * comps, comps), block]
                held[i, 0, v, :, block] = ((even + odd) * live).astype(BF16)
                held[i, 1, v, :, block] = ((even - odd) * live).astype(BF16)
        stores.append(
            pltpu.make_async_copy(held.at[:, :, :, :, block], out_ref.at[:, :, :, :, block], out_sem.at[n])
        )
        stores[-1].start()
    for store in stores:
        store.wait()


def kernel_params(mib):
    return pltpu.CompilerParams(vmem_limit_bytes=mib * 1024 * 1024)


def exchange(packed, bands):
    shaped = packed.reshape(bands, ROWS // 2, 2, LANES)
    return lax.all_to_all(shaped, "band", split_axis=0, concat_axis=0, tiled=True).reshape(packed.shape)


def in_hbm(*arrays):
    return [pltpu.with_memory_space_constraint(a, pltpu.HBM) for a in arrays]


def in_vmem(*arrays):
    return [pltpu.with_memory_space_constraint(a, pltpu.VMEM) for a in arrays]


def on_device(bands, fourier_in, row_points, gauss_weight, pair_order, legendre, diffusion):
    rows, _, levels, comps, orders = fourier_in.shape
    slots, nrows, half = legendre.shape
    group = 2 * levels * comps
    size = (bands * ROWS, LANES)
    message = pltpu.HBM(size, BF16)
    other = lax.ppermute(legendre, "lev", [(0, 1), (1, 0)])
    points, weights, listing, kappas = in_hbm(row_points, gauss_weight, pair_order, diffusion.T)
    packed = pl.pallas_call(
        pack_kernel,
        out_shape=message,
        in_specs=[ANY, SMEM, SMEM, VMEM],
        out_specs=ANY,
        scratch_shapes=[
            pltpu.VMEM(fourier_in.shape, BF16),
            pltpu.VMEM((orders, orders), BF16),
            pltpu.VMEM((group * rows, orders), F32),
            pltpu.VMEM(size, F32),
            pltpu.VMEM(size, BF16),
            pltpu.SemaphoreType.DMA((rows,)),
            pltpu.SemaphoreType.DMA((4,)),
        ],
        compiler_params=kernel_params(16),
        name="pack",
    )(*in_hbm(fourier_in), points, weights, listing)
    arrived = exchange(packed, bands)

    gain, selector = pl.pallas_call(
        between_kernel,
        out_shape=(
            jax.ShapeDtypeStruct((slots, 2 * group, orders + LANES), F32),
            pltpu.HBM((orders, orders), BF16),
        ),
        in_specs=[SMEM, SMEM, VMEM],
        out_specs=(VMEM, ANY),
        scratch_shapes=[pltpu.VMEM((orders, orders), BF16), pltpu.SemaphoreType.DMA(())],
        compiler_params=kernel_params(16),
        name="between",
    )(listing, kappas, listing)

    produced = pl.pallas_call(
        transform_kernel,
        out_shape=jax.ShapeDtypeStruct(size, BF16),
        in_specs=[VMEM, ANY, ANY, VMEM],
        out_specs=VMEM,
        scratch_shapes=[
            pltpu.VMEM(size, F32),
            pltpu.VMEM((3 * orders, LANES), F32),
            pltpu.VMEM((3 * LANES, orders), F32),
            pltpu.VMEM(legendre.shape, BF16),
            pltpu.VMEM(legendre.shape, BF16),
            pltpu.SemaphoreType.DMA((slots, 2)),
            pltpu.SemaphoreType.DMA((slots, 2)),
        ],
        compiler_params=kernel_params(40),
        name="transform",
    )(arrived, *in_hbm(legendre, other), gain)
    landed = exchange(produced, bands)
    return pl.pallas_call(
        unpack_kernel,
        out_shape=jax.ShapeDtypeStruct(fourier_in.shape, BF16),
        in_specs=[VMEM, SMEM, VMEM],
        out_specs=ANY,
        scratch_shapes=[
            pltpu.VMEM(size, F32),
            pltpu.VMEM((group * rows, orders), BF16),
            pltpu.VMEM((group * rows, orders), F32),
            pltpu.VMEM(fourier_in.shape, BF16),
            pltpu.SemaphoreType.DMA((orders // (2 * LANES),)),
        ],
        compiler_params=kernel_params(16),
        name="unpack",
    )(landed, points, *in_vmem(selector))


def solution(mesh):
    in_specs = (
        P("band", None, "lev", None, None),
        P("band"),
        P("band"),
        P(),
        P("band", None, "lev"),
        P(),
    )
    out_specs = P("band", None, "lev", None, None)
    return jax.shard_map(
        functools.partial(on_device, mesh.shape["band"]),
        mesh=mesh,
        in_specs=in_specs,
        out_specs=out_specs,
        check_vma=False,
    )
```

```python
import functools

import jax
import jax.numpy as jnp
from jax import lax
from jax.experimental import pallas as pl
from jax.experimental.pallas import tpu as pltpu
from jax.sharding import PartitionSpec as P

F32 = jnp.float32
BF16 = jnp.bfloat16
LANES = 128
HALF = LANES // 2
NT = (((1,), (1,)), ((), ()))
NN = (((1,), (0,)), ((), ()))
VMEM = pl.BlockSpec(memory_space=pltpu.VMEM)
SMEM = pl.BlockSpec(memory_space=pltpu.SMEM)
ANY = pl.BlockSpec(memory_space=pl.ANY)
TILES = 5
ROWS = 26
EARLY_SLOTS = (4, 0, 1)
LATE_SLOTS = (2, 3)


def dot(a, b, dims):
    return lax.dot_general(a, b, dims, preferred_element_type=F32)


def one_hot_rows(listing, slot, q, orders, bands):
    slots = listing.shape[1] // bands
    where_ = lax.broadcasted_iota(jnp.int32, (bands, listing.shape[1]), 1)
    owner = lax.broadcasted_iota(jnp.int32, (bands, listing.shape[1]), 0)
    lead = jnp.sum(jnp.where(where_ == owner * slots + slot, listing, 0), axis=1, keepdims=True)
    order = lead if q == 0 else orders - 1 - lead
    column = lax.broadcasted_iota(jnp.int32, (bands, orders), 1)
    return jnp.where(column == order, 1.0, 0.0).astype(BF16)


def cutoff_of(points, orders):
    return jnp.minimum(orders - 1, lax.shift_right_arithmetic(points - 1, 1))


def message_rows(wide, row, bands):
    return wide.at[pl.ds(row, bands, stride=ROWS), :]


def one_hot(listing_ref, sel_ref):
    orders = sel_ref.shape[1]
    bands = orders // (2 * TILES)
    listing = listing_ref[...].reshape(1, orders // 2)
    for j in range(TILES):
        for q in range(2):
            sel_ref[pl.ds((2 * j + q) * bands, bands), :] = one_hot_rows(listing, j, q, orders, bands)


def pack_kernel(
    x_ref,
    points_in,
    weight_in,
    order_in,
    kappa_in,
    listing_ref,
    table_ref,
    out_ref,
    sel_ref,
    gain_ref,
    held_ref,
    x_held,
    points_ref,
    weight_ref,
    order_ref,
    kappa_ref,
    fold,
    wide,
    x_sem,
    own_sem,
    table_sem,
):
    rows, _, levels, comps, orders = x_ref.shape
    bands = sel_ref.shape[0] // (2 * TILES)
    vc = levels * comps
    group = 2 * vc
    column = lax.broadcasted_iota(jnp.int32, (comps, orders), 1)
    scalars = [(points_in, points_ref), (weight_in, weight_ref), (order_in, order_ref), (kappa_in, kappa_ref)]
    small = [pltpu.make_async_copy(a, b, own_sem.at[n]) for n, (a, b) in enumerate(scalars)]
    loads = [pltpu.make_async_copy(x_ref.at[i], x_held.at[i], x_sem.at[i]) for i in range(rows)]
    table = [
        pltpu.make_async_copy(table_ref.at[j], held_ref.at[n], table_sem.at[n]) for n, j in enumerate(EARLY_SLOTS)
    ]
    for load in small + loads:
        load.start()
    one_hot(listing_ref, sel_ref)
    for load in small:
        load.wait()
    damping(order_ref, kappa_ref, gain_ref)
    for i in range(rows):
        live = (column <= cutoff_of(points_ref[i], orders)).astype(F32)
        factor = live * weight_ref[i]
        loads[i].wait()
        for v in range(levels):
            north = x_held[i, 0, v].astype(F32)
            south = x_held[i, 1, v].astype(F32)
            fold[pl.ds(i * group + v * comps, comps), :] = (north + south) * factor
            fold[pl.ds(i * group + vc + v * comps, comps), :] = (north - south) * factor
    for load in table:
        load.start()
    folded = fold[...].astype(BF16)
    per_tile = LANES // group
    for tile in range(3):
        first = tile * per_tile
        count = min(per_tile, 2 * TILES - first)
        sent = dot(folded, sel_ref[pl.ds(first * bands, count * bands), :], NT)

        def block(i):
            return [sent[i * group : (i + 1) * group, n * bands : (n + 1) * bands] for n in range(count)]

        for pair in range(rows // 2):
            if tile == 2:
                both = jnp.concatenate(block(2 * pair) + block(2 * pair + 1), axis=0)
                message_rows(wide, TILES * pair + 2, bands)[...] = jnp.transpose(both)
            else:
                for odd in range(2):
                    one = jnp.concatenate(block(2 * pair + odd), axis=0)
                    message_rows(wide, TILES * pair + 3 * odd + tile, bands)[...] = jnp.transpose(one)
    message_rows(wide, ROWS - 1, bands)[...] = jnp.zeros((bands, LANES), F32)
    out_ref[...] = wide[...].astype(BF16)
    for load in table:
        load.wait()


def damping(order_ref, kappa_ref, gain_ref):
    slots = gain_ref.shape[0]
    orders = gain_ref.shape[2] - LANES
    levels = kappa_ref.shape[1] // 2
    vc = 4 * levels
    band = lax.axis_index("band")
    lev = lax.axis_index("lev")
    which = lax.broadcasted_iota(jnp.int32, (vc, 1), 0)
    kappa = jnp.zeros((vc, 1), F32)
    for n in range(2 * levels):
        kappa = jnp.where(lax.shift_right_logical(which, 1) == n, kappa_ref[n % 2, lev * levels + n // 2], kappa)
    row = lax.broadcasted_iota(jnp.int32, (1, gain_ref.shape[2]), 1)
    odd = row > orders // 2
    odd_number = odd.astype(jnp.int32)
    position = row - odd_number * (orders // 2 + 1)
    for j in range(slots):
        first_order = order_ref[band * slots + j]
        second_order = orders - 1 - first_order
        boundary = jnp.where(
            odd,
            lax.shift_right_arithmetic(orders - first_order, 1),
            lax.shift_right_arithmetic(orders + 1 - first_order, 1),
        )
        leading = position < boundary
        degree = jnp.where(
            leading,
            first_order + odd_number + 2 * position,
            second_order + odd_number + 2 * (position - boundary),
        )
        growth = (degree * (degree + 1)).astype(F32) / float(orders * (orders + 1))
        factor = 1.0 / (1.0 + kappa * growth)
        for q in range(2):
            for p in range(2):
                mask = jnp.logical_and(
                    leading if q == 0 else jnp.logical_not(leading), odd if p == 1 else jnp.logical_not(odd)
                )
                gain_ref[j, pl.ds((2 * q + p) * vc, vc), :] = jnp.where(mask, factor, 0.0)


def transform_kernel(got_ref, early_ref, table_ref, other_ref, gain_ref, out_ref, late_ref, wide, grid, back, late_sem):
    slots, nrows, half = other_ref.shape
    orders = nrows - 1
    bands = got_ref.shape[0] // ROWS
    rows = orders // bands
    four = gain_ref.shape[1]
    lev = lax.axis_index("lev")
    own_first = pl.multiple_of(lev * half, LANES)
    other_first = pl.multiple_of((1 - lev) * half, LANES)

    loads = {
        j: pltpu.make_async_copy(table_ref.at[j], late_ref.at[n], late_sem.at[n]) for n, j in enumerate(LATE_SLOTS)
    }
    for load in loads.values():
        load.start()

    def own_table(j):
        return early_ref.at[EARLY_SLOTS.index(j)] if j in EARLY_SLOTS else late_ref.at[LATE_SLOTS.index(j)]

    def latitude(i, tile):
        return grid.at[pl.ds(tile * orders + i, bands, stride=rows), :]

    wide[...] = got_ref[...].astype(F32)
    right = lax.broadcasted_iota(jnp.int32, (bands, LANES), 1) >= HALF
    second = lax.broadcasted_iota(jnp.int32, (orders, LANES), 1) >= HALF
    columns, coeffs, ends, chosen, chosen_last = {}, {}, {}, {}, {}

    def arrange(tile):
        for pair in range(rows // 2):
            for odd in range(2):
                part = message_rows(wide, TILES * pair + (2 if tile == 2 else 3 * odd + tile), bands)[...]
                latitude(2 * pair + odd, tile)[...] = pltpu.roll(part, HALF, 1) if tile == 2 and odd else part
        columns[tile] = [
            grid[pl.ds(tile * orders + first, half), :].astype(BF16) for first in (own_first, other_first)
        ]

    def forward(j):
        own, other = columns[j // 2]
        partial = dot(other_ref[j, :orders, :], other, NN)
        if j in loads:
            loads[j].wait()
        table = own_table(j)
        coeffs[j] = dot(table[:orders, :], own, NN) + partial
        ends[j] = dot(table[pl.ds(orders, 1), :], own, NN) + dot(other_ref[j, pl.ds(orders, 1), :], other, NN)

    def settle(tile):
        inside = [j for j in (2 * tile, 2 * tile + 1) if j < slots]
        both = coeffs[inside[0]] if len(inside) == 1 else jnp.where(second, coeffs[inside[1]], coeffs[inside[0]])
        turned = jnp.transpose(both)
        rest = jnp.zeros((8 - len(inside), LANES), F32)
        turned_ends = jnp.transpose(jnp.concatenate([ends[j] for j in inside] + [rest], axis=0))
        for n, j in enumerate(inside):
            mine = slice(n * four, (n + 1) * four)
            chosen[j] = (turned[mine] * gain_ref[j, :, pl.ds(0, orders)]).astype(BF16)
            chosen_last[j] = (turned_ends[mine, n : n + 1] * gain_ref[j, :, pl.ds(orders, 1)]).astype(BF16).astype(F32)

    def inverse(j):
        for table, first in ((own_table(j), own_first), (other_ref.at[j], other_first)):
            last = chosen_last[j] * table[pl.ds(orders, 1), :].astype(F32)
            back[pl.ds(j * four, four), pl.ds(first, half)] = dot(chosen[j], table[:orders, :], NN) + last

    def finish(tile):
        grid[pl.ds(tile * orders, orders), :] = jnp.transpose(back[pl.ds(tile * LANES, LANES), :])
        for pair in range(rows // 2):
            even, odd = latitude(2 * pair, tile)[...], latitude(2 * pair + 1, tile)[...]
            if tile == 2:
                both = jnp.where(right, pltpu.roll(odd, HALF, 1), even)
                message_rows(wide, TILES * pair + 2, bands)[...] = both
            else:
                message_rows(wide, TILES * pair + tile, bands)[...] = even
                message_rows(wide, TILES * pair + 3 + tile, bands)[...] = odd

    arrange(2)
    arrange(0)
    forward(4)
    forward(0)
    settle(2)
    inverse(4)
    forward(1)
    arrange(1)
    finish(2)
    forward(2)
    settle(0)
    inverse(0)
    forward(3)
    inverse(1)
    finish(0)
    settle(1)
    inverse(2)
    inverse(3)
    finish(1)
    message_rows(wide, ROWS - 1, bands)[...] = jnp.zeros((bands, LANES), F32)
    out_ref[...] = wide[...].astype(BF16)


def unpack_kernel(got_ref, points_ref, sel_ref, out_ref, wide, gathered, placed, held, out_sem):
    rows, _, levels, comps, orders = out_ref.shape
    bands = got_ref.shape[0] // ROWS
    vc = levels * comps
    group = 2 * vc
    per_tile = LANES // group
    wide[...] = got_ref[...].astype(F32)
    for pair in range(rows // 2):
        parts = [jnp.transpose(message_rows(wide, TILES * pair + u, bands)[...]).astype(BF16) for u in range(TILES)]
        for odd in range(2):
            tiles = [parts[3 * odd], parts[3 * odd + 1], parts[2][odd * HALF : (odd + 1) * HALF]]
            for n in range(2 * TILES):
                at = (n % per_tile) * group
                gathered[pl.ds((2 * pair + odd) * group, group), pl.ds(n * bands, bands)] = tiles[n // per_tile][
                    at : at + group
                ]
    width = 2 * LANES
    stores = []
    for n in range(orders // width):
        block = pl.ds(n * width, width)
        placed[:, block] = dot(gathered[...], sel_ref[:, block], NN)
        column = n * width + lax.broadcasted_iota(jnp.int32, (comps, width), 1)
        for i in range(rows):
            live = (column <= cutoff_of(points_ref[i], orders)).astype(F32)
            for v in range(levels):
                even = placed[pl.ds(i * group + v * comps, comps), block]
                odd = placed[pl.ds(i * group + vc + v * comps, comps), block]
                held[i, 0, v, :, block] = ((even + odd) * live).astype(BF16)
                held[i, 1, v, :, block] = ((even - odd) * live).astype(BF16)
        stores.append(
            pltpu.make_async_copy(held.at[:, :, :, :, block], out_ref.at[:, :, :, :, block], out_sem.at[n])
        )
        stores[-1].start()
    for store in stores:
        store.wait()


def kernel_params(mib):
    return pltpu.CompilerParams(vmem_limit_bytes=mib * 1024 * 1024)


def exchange(packed, bands):
    shaped = packed.reshape(bands, ROWS // 2, 2, LANES)
    return lax.all_to_all(shaped, "band", split_axis=0, concat_axis=0, tiled=True).reshape(packed.shape)


def in_hbm(*arrays):
    return [pltpu.with_memory_space_constraint(a, pltpu.HBM) for a in arrays]


def in_vmem(*arrays):
    return [pltpu.with_memory_space_constraint(a, pltpu.VMEM) for a in arrays]


def on_device(bands, fourier_in, row_points, gauss_weight, pair_order, legendre, diffusion):
    rows, _, levels, comps, orders = fourier_in.shape
    slots, nrows, half = legendre.shape
    group = 2 * levels * comps
    size = (bands * ROWS, LANES)
    other = lax.ppermute(legendre, "lev", [(0, 1), (1, 0)])
    points, weights, order, kappas = in_hbm(row_points, gauss_weight, pair_order, diffusion.T)
    packed, selector, gain, early = pl.pallas_call(
        pack_kernel,
        out_shape=(
            pltpu.VMEM(size, BF16),
            pltpu.VMEM((orders, orders), BF16),
            pltpu.VMEM((slots, 2 * group, orders + LANES), F32),
            pltpu.VMEM((len(EARLY_SLOTS), nrows, half), BF16),
        ),
        in_specs=[ANY, ANY, ANY, ANY, ANY, VMEM, ANY],
        out_specs=(VMEM,) * 4,
        scratch_shapes=[
            pltpu.VMEM(fourier_in.shape, BF16),
            pltpu.SMEM(row_points.shape, jnp.int32),
            pltpu.SMEM(gauss_weight.shape, F32),
            pltpu.SMEM(pair_order.shape, jnp.int32),
            pltpu.SMEM(diffusion.shape[::-1], F32),
            pltpu.VMEM((group * rows, orders), F32),
            pltpu.VMEM(size, F32),
            pltpu.SemaphoreType.DMA((rows,)),
            pltpu.SemaphoreType.DMA((4,)),
            pltpu.SemaphoreType.DMA((len(EARLY_SLOTS),)),
        ],
        compiler_params=kernel_params(16),
        name="pack",
    )(*in_hbm(fourier_in), points, weights, order, kappas, order, *in_hbm(legendre))
    arrived = exchange(packed, bands)

    produced = pl.pallas_call(
        transform_kernel,
        out_shape=jax.ShapeDtypeStruct(size, BF16),
        in_specs=[VMEM, VMEM, ANY, VMEM, VMEM],
        out_specs=VMEM,
        scratch_shapes=[
            pltpu.VMEM((len(LATE_SLOTS), nrows, half), BF16),
            pltpu.VMEM(size, F32),
            pltpu.VMEM((3 * orders, LANES), F32),
            pltpu.VMEM((3 * LANES, orders), F32),
            pltpu.SemaphoreType.DMA((len(LATE_SLOTS),)),
        ],
        compiler_params=kernel_params(20),
        name="transform",
    )(arrived, *in_vmem(early), *in_hbm(legendre), *in_vmem(other, gain))
    landed = exchange(produced, bands)
    return pl.pallas_call(
        unpack_kernel,
        out_shape=jax.ShapeDtypeStruct(fourier_in.shape, BF16),
        in_specs=[VMEM, SMEM, VMEM],
        out_specs=ANY,
        scratch_shapes=[
            pltpu.VMEM(size, F32),
            pltpu.VMEM((group * rows, orders), BF16),
            pltpu.VMEM((group * rows, orders), F32),
            pltpu.VMEM(fourier_in.shape, BF16),
            pltpu.SemaphoreType.DMA((orders // (2 * LANES),)),
        ],
        compiler_params=kernel_params(16),
        name="unpack",
    )(landed, points, *in_vmem(selector))


def solution(mesh):
    in_specs = (
        P("band", None, "lev", None, None),
        P("band"),
        P("band"),
        P(),
        P("band", None, "lev"),
        P(),
    )
    out_specs = P("band", None, "lev", None, None)
    return jax.shard_map(
        functools.partial(on_device, mesh.shape["band"]),
        mesh=mesh,
        in_specs=in_specs,
        out_specs=out_specs,
        check_vma=False,
    )
```

```python
import functools

import jax
import jax.numpy as jnp
from jax import lax
from jax.experimental import pallas as pl
from jax.experimental.pallas import tpu as pltpu
from jax.sharding import PartitionSpec as P

F32 = jnp.float32
BF16 = jnp.bfloat16
LANES = 128
HALF = LANES // 2
NT = (((1,), (1,)), ((), ()))
NN = (((1,), (0,)), ((), ()))
VMEM = pl.BlockSpec(memory_space=pltpu.VMEM)
SMEM = pl.BlockSpec(memory_space=pltpu.SMEM)
ANY = pl.BlockSpec(memory_space=pl.ANY)
TILES = 5
ROWS = 26
EARLY_SLOTS = (4, 0, 1)
LATE_SLOTS = (2, 3)


def dot(a, b, dims):
    return lax.dot_general(a, b, dims, preferred_element_type=F32)


def one_hot_rows(listing, slot, q, orders, bands):
    slots = listing.shape[1] // bands
    where_ = lax.broadcasted_iota(jnp.int32, (bands, listing.shape[1]), 1)
    owner = lax.broadcasted_iota(jnp.int32, (bands, listing.shape[1]), 0)
    lead = jnp.sum(jnp.where(where_ == owner * slots + slot, listing, 0), axis=1, keepdims=True)
    order = lead if q == 0 else orders - 1 - lead
    column = lax.broadcasted_iota(jnp.int32, (bands, orders), 1)
    return jnp.where(column == order, 1.0, 0.0).astype(BF16)


def cutoff_of(points, orders):
    return jnp.minimum(orders - 1, lax.shift_right_arithmetic(points - 1, 1))


def message_rows(wide, row, bands):
    return wide.at[pl.ds(row, bands, stride=ROWS), :]


def one_hot(listing_ref, sel_ref):
    orders = sel_ref.shape[1]
    bands = orders // (2 * TILES)
    listing = listing_ref[...].reshape(1, orders // 2)
    for j in range(TILES):
        for q in range(2):
            sel_ref[pl.ds((2 * j + q) * bands, bands), :] = one_hot_rows(listing, j, q, orders, bands)


def pack_kernel(
    x_ref,
    points_in,
    weight_in,
    order_in,
    kappa_in,
    listing_ref,
    table_ref,
    out_ref,
    sel_ref,
    gain_ref,
    held_ref,
    x_held,
    points_ref,
    weight_ref,
    order_ref,
    kappa_ref,
    fold,
    wide,
    x_sem,
    own_sem,
    table_sem,
):
    rows, _, levels, comps, orders = x_ref.shape
    bands = sel_ref.shape[0] // (2 * TILES)
    vc = levels * comps
    group = 2 * vc
    column = lax.broadcasted_iota(jnp.int32, (comps, orders), 1)
    scalars = [(points_in, points_ref), (weight_in, weight_ref), (order_in, order_ref), (kappa_in, kappa_ref)]
    small = [pltpu.make_async_copy(a, b, own_sem.at[n]) for n, (a, b) in enumerate(scalars)]
    loads = [pltpu.make_async_copy(x_ref.at[i], x_held.at[i], x_sem.at[i]) for i in range(rows)]
    table = [
        pltpu.make_async_copy(table_ref.at[j], held_ref.at[n], table_sem.at[n]) for n, j in enumerate(EARLY_SLOTS)
    ]
    for load in small + loads:
        load.start()
    one_hot(listing_ref, sel_ref)
    for load in small:
        load.wait()
    for load in table:
        load.start()
    damping(order_ref, kappa_ref, gain_ref)
    for i in range(rows):
        live = (column <= cutoff_of(points_ref[i], orders)).astype(F32)
        factor = live * weight_ref[i]
        loads[i].wait()
        for v in range(levels):
            north = x_held[i, 0, v].astype(F32)
            south = x_held[i, 1, v].astype(F32)
            fold[pl.ds(i * group + v * comps, comps), :] = (north + south) * factor
            fold[pl.ds(i * group + vc + v * comps, comps), :] = (north - south) * factor
    folded = fold[...].astype(BF16)
    per_tile = LANES // group
    for tile in range(3):
        first = tile * per_tile
        count = min(per_tile, 2 * TILES - first)
        sent = dot(folded, sel_ref[pl.ds(first * bands, count * bands), :], NT)

        def block(i):
            return [sent[i * group : (i + 1) * group, n * bands : (n + 1) * bands] for n in range(count)]

        for pair in range(rows // 2):
            if tile == 2:
                both = jnp.concatenate(block(2 * pair) + block(2 * pair + 1), axis=0)
                message_rows(wide, TILES * pair + 2, bands)[...] = jnp.transpose(both)
            else:
                for odd in range(2):
                    one = jnp.concatenate(block(2 * pair + odd), axis=0)
                    message_rows(wide, TILES * pair + 3 * odd + tile, bands)[...] = jnp.transpose(one)
    message_rows(wide, ROWS - 1, bands)[...] = jnp.zeros((bands, LANES), F32)
    out_ref[...] = wide[...].astype(BF16)
    for load in table:
        load.wait()


def damping(order_ref, kappa_ref, gain_ref):
    slots = gain_ref.shape[0]
    orders = gain_ref.shape[2] - LANES
    levels = kappa_ref.shape[1] // 2
    vc = 4 * levels
    band = lax.axis_index("band")
    lev = lax.axis_index("lev")
    which = lax.broadcasted_iota(jnp.int32, (vc, 1), 0)
    kappa = jnp.zeros((vc, 1), F32)
    for n in range(2 * levels):
        kappa = jnp.where(lax.shift_right_logical(which, 1) == n, kappa_ref[n % 2, lev * levels + n // 2], kappa)
    row = lax.broadcasted_iota(jnp.int32, (1, gain_ref.shape[2]), 1)
    odd = row > orders // 2
    odd_number = odd.astype(jnp.int32)
    position = row - odd_number * (orders // 2 + 1)
    for j in range(slots):
        first_order = order_ref[band * slots + j]
        second_order = orders - 1 - first_order
        boundary = jnp.where(
            odd,
            lax.shift_right_arithmetic(orders - first_order, 1),
            lax.shift_right_arithmetic(orders + 1 - first_order, 1),
        )
        leading = position < boundary
        degree = jnp.where(
            leading,
            first_order + odd_number + 2 * position,
            second_order + odd_number + 2 * (position - boundary),
        )
        growth = (degree * (degree + 1)).astype(F32) / float(orders * (orders + 1))
        factor = 1.0 / (1.0 + kappa * growth)
        for q in range(2):
            for p in range(2):
                mask = jnp.logical_and(
                    leading if q == 0 else jnp.logical_not(leading), odd if p == 1 else jnp.logical_not(odd)
                )
                gain_ref[j, pl.ds((2 * q + p) * vc, vc), :] = jnp.where(mask, factor, 0.0)


def transform_kernel(got_ref, early_ref, table_ref, other_ref, gain_ref, out_ref, late_ref, wide, grid, back, late_sem):
    slots, nrows, half = other_ref.shape
    orders = nrows - 1
    bands = got_ref.shape[0] // ROWS
    rows = orders // bands
    four = gain_ref.shape[1]
    lev = lax.axis_index("lev")
    own_first = pl.multiple_of(lev * half, LANES)
    other_first = pl.multiple_of((1 - lev) * half, LANES)

    loads = {
        j: pltpu.make_async_copy(table_ref.at[j], late_ref.at[n], late_sem.at[n]) for n, j in enumerate(LATE_SLOTS)
    }
    for load in loads.values():
        load.start()

    def own_table(j):
        return early_ref.at[EARLY_SLOTS.index(j)] if j in EARLY_SLOTS else late_ref.at[LATE_SLOTS.index(j)]

    def latitude(i, tile):
        return grid.at[pl.ds(tile * orders + i, bands, stride=rows), :]

    wide[...] = got_ref[...].astype(F32)
    right = lax.broadcasted_iota(jnp.int32, (bands, LANES), 1) >= HALF
    second = lax.broadcasted_iota(jnp.int32, (orders, LANES), 1) >= HALF
    columns, coeffs, ends, chosen, chosen_last = {}, {}, {}, {}, {}

    def arrange(tile):
        for pair in range(rows // 2):
            for odd in range(2):
                part = message_rows(wide, TILES * pair + (2 if tile == 2 else 3 * odd + tile), bands)[...]
                latitude(2 * pair + odd, tile)[...] = pltpu.roll(part, HALF, 1) if tile == 2 and odd else part
        columns[tile] = [
            grid[pl.ds(tile * orders + first, half), :].astype(BF16) for first in (own_first, other_first)
        ]

    def forward(j):
        own, other = columns[j // 2]
        if j in loads:
            loads[j].wait()
        table = own_table(j)
        coeffs[j] = dot(table[:orders, :], own, NN) + dot(other_ref[j, :orders, :], other, NN)
        ends[j] = dot(table[pl.ds(orders, 1), :], own, NN) + dot(other_ref[j, pl.ds(orders, 1), :], other, NN)

    def settle(tile):
        inside = [j for j in (2 * tile, 2 * tile + 1) if j < slots]
        both = coeffs[inside[0]] if len(inside) == 1 else jnp.where(second, coeffs[inside[1]], coeffs[inside[0]])
        turned = jnp.transpose(both)
        rest = jnp.zeros((8 - len(inside), LANES), F32)
        turned_ends = jnp.transpose(jnp.concatenate([ends[j] for j in inside] + [rest], axis=0))
        for n, j in enumerate(inside):
            mine = slice(n * four, (n + 1) * four)
            chosen[j] = (turned[mine] * gain_ref[j, :, pl.ds(0, orders)]).astype(BF16)
            chosen_last[j] = (turned_ends[mine, n : n + 1] * gain_ref[j, :, pl.ds(orders, 1)]).astype(BF16).astype(F32)

    def inverse(j):
        for table, first in ((own_table(j), own_first), (other_ref.at[j], other_first)):
            last = chosen_last[j] * table[pl.ds(orders, 1), :].astype(F32)
            back[pl.ds(j * four, four), pl.ds(first, half)] = dot(chosen[j], table[:orders, :], NN) + last

    def finish(tile):
        grid[pl.ds(tile * orders, orders), :] = jnp.transpose(back[pl.ds(tile * LANES, LANES), :])
        for pair in range(rows // 2):
            even, odd = latitude(2 * pair, tile)[...], latitude(2 * pair + 1, tile)[...]
            if tile == 2:
                both = jnp.where(right, pltpu.roll(odd, HALF, 1), even)
                message_rows(wide, TILES * pair + 2, bands)[...] = both
            else:
                message_rows(wide, TILES * pair + tile, bands)[...] = even
                message_rows(wide, TILES * pair + 3 + tile, bands)[...] = odd

    arrange(2)
    arrange(0)
    forward(4)
    forward(0)
    settle(2)
    inverse(4)
    forward(1)
    arrange(1)
    finish(2)
    forward(2)
    settle(0)
    inverse(0)
    forward(3)
    inverse(1)
    finish(0)
    settle(1)
    inverse(2)
    inverse(3)
    finish(1)
    message_rows(wide, ROWS - 1, bands)[...] = jnp.zeros((bands, LANES), F32)
    out_ref[...] = wide[...].astype(BF16)


def unpack_kernel(got_ref, points_ref, sel_ref, out_ref, wide, gathered, placed, held, out_sem):
    rows, _, levels, comps, orders = out_ref.shape
    bands = got_ref.shape[0] // ROWS
    vc = levels * comps
    group = 2 * vc
    per_tile = LANES // group
    wide[...] = got_ref[...].astype(F32)
    for pair in range(rows // 2):
        parts = [jnp.transpose(message_rows(wide, TILES * pair + u, bands)[...]).astype(BF16) for u in range(TILES)]
        for odd in range(2):
            tiles = [parts[3 * odd], parts[3 * odd + 1], parts[2][odd * HALF : (odd + 1) * HALF]]
            for n in range(2 * TILES):
                at = (n % per_tile) * group
                gathered[pl.ds((2 * pair + odd) * group, group), pl.ds(n * bands, bands)] = tiles[n // per_tile][
                    at : at + group
                ]
    column = lax.broadcasted_iota(jnp.int32, (comps, orders), 1)
    cut = rows // 2 * group
    stores = []
    for i in range(rows):
        if i in (0, rows // 2):
            lines = pl.ds(i * group, cut)
            placed[lines, :] = dot(gathered[lines, :], sel_ref[...], NN)
        live = (column <= cutoff_of(points_ref[i], orders)).astype(F32)
        for v in range(levels):
            even = placed[pl.ds(i * group + v * comps, comps), :]
            odd = placed[pl.ds(i * group + vc + v * comps, comps), :]
            held[i, 0, v] = ((even + odd) * live).astype(BF16)
            held[i, 1, v] = ((even - odd) * live).astype(BF16)
        stores.append(pltpu.make_async_copy(held.at[i], out_ref.at[i], out_sem.at[i]))
        stores[-1].start()
    for store in stores:
        store.wait()


def kernel_params(mib):
    return pltpu.CompilerParams(vmem_limit_bytes=mib * 1024 * 1024)


def exchange(packed, bands):
    shaped = packed.reshape(bands, ROWS // 2, 2, LANES)
    return lax.all_to_all(shaped, "band", split_axis=0, concat_axis=0, tiled=True).reshape(packed.shape)


def in_hbm(*arrays):
    return [pltpu.with_memory_space_constraint(a, pltpu.HBM) for a in arrays]


def in_vmem(*arrays):
    return [pltpu.with_memory_space_constraint(a, pltpu.VMEM) for a in arrays]


def on_device(bands, fourier_in, row_points, gauss_weight, pair_order, legendre, diffusion):
    rows, _, levels, comps, orders = fourier_in.shape
    slots, nrows, half = legendre.shape
    group = 2 * levels * comps
    size = (bands * ROWS, LANES)
    other = lax.ppermute(legendre, "lev", [(0, 1), (1, 0)])
    points, weights, order, kappas = in_hbm(row_points, gauss_weight, pair_order, diffusion.T)
    packed, selector, gain, early = pl.pallas_call(
        pack_kernel,
        out_shape=(
            pltpu.VMEM(size, BF16),
            pltpu.VMEM((orders, orders), BF16),
            pltpu.VMEM((slots, 2 * group, orders + LANES), F32),
            pltpu.VMEM((len(EARLY_SLOTS), nrows, half), BF16),
        ),
        in_specs=[ANY, ANY, ANY, ANY, ANY, VMEM, ANY],
        out_specs=(VMEM,) * 4,
        scratch_shapes=[
            pltpu.VMEM(fourier_in.shape, BF16),
            pltpu.SMEM(row_points.shape, jnp.int32),
            pltpu.SMEM(gauss_weight.shape, F32),
            pltpu.SMEM(pair_order.shape, jnp.int32),
            pltpu.SMEM(diffusion.shape[::-1], F32),
            pltpu.VMEM((group * rows, orders), F32),
            pltpu.VMEM(size, F32),
            pltpu.SemaphoreType.DMA((rows,)),
            pltpu.SemaphoreType.DMA((4,)),
            pltpu.SemaphoreType.DMA((len(EARLY_SLOTS),)),
        ],
        compiler_params=kernel_params(16),
        name="pack",
    )(*in_hbm(fourier_in), points, weights, order, kappas, order, *in_hbm(legendre))
    arrived = exchange(packed, bands)

    produced = pl.pallas_call(
        transform_kernel,
        out_shape=jax.ShapeDtypeStruct(size, BF16),
        in_specs=[VMEM, VMEM, ANY, VMEM, VMEM],
        out_specs=VMEM,
        scratch_shapes=[
            pltpu.VMEM((len(LATE_SLOTS), nrows, half), BF16),
            pltpu.VMEM(size, F32),
            pltpu.VMEM((3 * orders, LANES), F32),
            pltpu.VMEM((3 * LANES, orders), F32),
            pltpu.SemaphoreType.DMA((len(LATE_SLOTS),)),
        ],
        compiler_params=kernel_params(20),
        name="transform",
    )(arrived, *in_vmem(early), *in_hbm(legendre), *in_vmem(other, gain))
    landed = exchange(produced, bands)
    return pl.pallas_call(
        unpack_kernel,
        out_shape=jax.ShapeDtypeStruct(fourier_in.shape, BF16),
        in_specs=[VMEM, SMEM, VMEM],
        out_specs=ANY,
        scratch_shapes=[
            pltpu.VMEM(size, F32),
            pltpu.VMEM((group * rows, orders), BF16),
            pltpu.VMEM((group * rows, orders), F32),
            pltpu.VMEM(fourier_in.shape, BF16),
            pltpu.SemaphoreType.DMA((rows,)),
        ],
        compiler_params=kernel_params(16),
        name="unpack",
    )(landed, points, *in_vmem(selector))


def solution(mesh):
    in_specs = (
        P("band", None, "lev", None, None),
        P("band"),
        P("band"),
        P(),
        P("band", None, "lev"),
        P(),
    )
    out_specs = P("band", None, "lev", None, None)
    return jax.shard_map(
        functools.partial(on_device, mesh.shape["band"]),
        mesh=mesh,
        in_specs=in_specs,
        out_specs=out_specs,
        check_vma=False,
    )
```

```python
import functools

import jax
import jax.numpy as jnp
from jax import lax
from jax.experimental import pallas as pl
from jax.experimental.pallas import tpu as pltpu
from jax.sharding import PartitionSpec as P

F32 = jnp.float32
BF16 = jnp.bfloat16
LANES = 128
HALF = LANES // 2
NT = (((1,), (1,)), ((), ()))
NN = (((1,), (0,)), ((), ()))
VMEM = pl.BlockSpec(memory_space=pltpu.VMEM)
SMEM = pl.BlockSpec(memory_space=pltpu.SMEM)
ANY = pl.BlockSpec(memory_space=pl.ANY)
TILES = 5
ROWS = 26
EARLY_SLOTS = (4, 0)
LATE_SLOTS = (1, 2, 3)


def dot(a, b, dims):
    return lax.dot_general(a, b, dims, preferred_element_type=F32)


def one_hot_rows(listing, slot, q, orders, bands):
    slots = listing.shape[1] // bands
    where_ = lax.broadcasted_iota(jnp.int32, (bands, listing.shape[1]), 1)
    owner = lax.broadcasted_iota(jnp.int32, (bands, listing.shape[1]), 0)
    lead = jnp.sum(jnp.where(where_ == owner * slots + slot, listing, 0), axis=1, keepdims=True)
    order = lead if q == 0 else orders - 1 - lead
    column = lax.broadcasted_iota(jnp.int32, (bands, orders), 1)
    return jnp.where(column == order, 1.0, 0.0).astype(BF16)


def cutoff_of(points, orders):
    return jnp.minimum(orders - 1, lax.shift_right_arithmetic(points - 1, 1))


def message_rows(wide, row, bands):
    return wide.at[pl.ds(row, bands, stride=ROWS), :]


def one_hot(listing_ref, sel_ref):
    orders = sel_ref.shape[1]
    bands = orders // (2 * TILES)
    listing = listing_ref[...].reshape(1, orders // 2)
    for j in range(TILES):
        for q in range(2):
            sel_ref[pl.ds((2 * j + q) * bands, bands), :] = one_hot_rows(listing, j, q, orders, bands)


def pack_kernel(
    x_ref,
    points_in,
    weight_in,
    order_in,
    kappa_in,
    listing_ref,
    table_ref,
    out_ref,
    sel_ref,
    gain_ref,
    held_ref,
    x_held,
    points_ref,
    weight_ref,
    order_ref,
    kappa_ref,
    fold,
    wide,
    x_sem,
    own_sem,
    table_sem,
):
    rows, _, levels, comps, orders = x_ref.shape
    bands = sel_ref.shape[0] // (2 * TILES)
    vc = levels * comps
    group = 2 * vc
    column = lax.broadcasted_iota(jnp.int32, (comps, orders), 1)
    scalars = [(points_in, points_ref), (weight_in, weight_ref), (order_in, order_ref), (kappa_in, kappa_ref)]
    small = [pltpu.make_async_copy(a, b, own_sem.at[n]) for n, (a, b) in enumerate(scalars)]
    loads = [pltpu.make_async_copy(x_ref.at[i], x_held.at[i], x_sem.at[i]) for i in range(rows)]
    table = [
        pltpu.make_async_copy(table_ref.at[j], held_ref.at[n], table_sem.at[n]) for n, j in enumerate(EARLY_SLOTS)
    ]
    for load in small + loads:
        load.start()
    one_hot(listing_ref, sel_ref)
    for load in small:
        load.wait()
    for load in table:
        load.start()
    damping(order_ref, kappa_ref, gain_ref)
    for i in range(rows):
        live = (column <= cutoff_of(points_ref[i], orders)).astype(F32)
        factor = live * weight_ref[i]
        loads[i].wait()
        for v in range(levels):
            north = x_held[i, 0, v].astype(F32)
            south = x_held[i, 1, v].astype(F32)
            fold[pl.ds(i * group + v * comps, comps), :] = (north + south) * factor
            fold[pl.ds(i * group + vc + v * comps, comps), :] = (north - south) * factor
    folded = fold[...].astype(BF16)
    per_tile = LANES // group
    for tile in range(3):
        first = tile * per_tile
        count = min(per_tile, 2 * TILES - first)
        sent = dot(folded, sel_ref[pl.ds(first * bands, count * bands), :], NT)

        def block(i):
            return [sent[i * group : (i + 1) * group, n * bands : (n + 1) * bands] for n in range(count)]

        for pair in range(rows // 2):
            if tile == 2:
                both = jnp.concatenate(block(2 * pair) + block(2 * pair + 1), axis=0)
                message_rows(wide, TILES * pair + 2, bands)[...] = jnp.transpose(both)
            else:
                for odd in range(2):
                    one = jnp.concatenate(block(2 * pair + odd), axis=0)
                    message_rows(wide, TILES * pair + 3 * odd + tile, bands)[...] = jnp.transpose(one)
    message_rows(wide, ROWS - 1, bands)[...] = jnp.zeros((bands, LANES), F32)
    out_ref[...] = wide[...].astype(BF16)
    for load in table:
        load.wait()


def damping(order_ref, kappa_ref, gain_ref):
    slots = gain_ref.shape[0]
    orders = gain_ref.shape[2] - LANES
    levels = kappa_ref.shape[1] // 2
    vc = 4 * levels
    band = lax.axis_index("band")
    lev = lax.axis_index("lev")
    which = lax.broadcasted_iota(jnp.int32, (vc, 1), 0)
    kappa = jnp.zeros((vc, 1), F32)
    for n in range(2 * levels):
        kappa = jnp.where(lax.shift_right_logical(which, 1) == n, kappa_ref[n % 2, lev * levels + n // 2], kappa)
    row = lax.broadcasted_iota(jnp.int32, (1, gain_ref.shape[2]), 1)
    odd = row > orders // 2
    odd_number = odd.astype(jnp.int32)
    position = row - odd_number * (orders // 2 + 1)
    for j in range(slots):
        first_order = order_ref[band * slots + j]
        second_order = orders - 1 - first_order
        boundary = jnp.where(
            odd,
            lax.shift_right_arithmetic(orders - first_order, 1),
            lax.shift_right_arithmetic(orders + 1 - first_order, 1),
        )
        leading = position < boundary
        degree = jnp.where(
            leading,
            first_order + odd_number + 2 * position,
            second_order + odd_number + 2 * (position - boundary),
        )
        growth = (degree * (degree + 1)).astype(F32) / float(orders * (orders + 1))
        factor = 1.0 / (1.0 + kappa * growth)
        for q in range(2):
            for p in range(2):
                mask = jnp.logical_and(
                    leading if q == 0 else jnp.logical_not(leading), odd if p == 1 else jnp.logical_not(odd)
                )
                gain_ref[j, pl.ds((2 * q + p) * vc, vc), :] = jnp.where(mask, factor, 0.0)


def transform_kernel(got_ref, early_ref, table_ref, other_ref, gain_ref, out_ref, late_ref, wide, grid, back, late_sem):
    slots, nrows, half = other_ref.shape
    orders = nrows - 1
    bands = got_ref.shape[0] // ROWS
    rows = orders // bands
    four = gain_ref.shape[1]
    lev = lax.axis_index("lev")
    own_first = pl.multiple_of(lev * half, LANES)
    other_first = pl.multiple_of((1 - lev) * half, LANES)

    loads = {
        j: pltpu.make_async_copy(table_ref.at[j], late_ref.at[n], late_sem.at[n]) for n, j in enumerate(LATE_SLOTS)
    }
    for load in loads.values():
        load.start()

    def own_table(j):
        return early_ref.at[EARLY_SLOTS.index(j)] if j in EARLY_SLOTS else late_ref.at[LATE_SLOTS.index(j)]

    def latitude(i, tile):
        return grid.at[pl.ds(tile * orders + i, bands, stride=rows), :]

    wide[...] = got_ref[...].astype(F32)
    right = lax.broadcasted_iota(jnp.int32, (bands, LANES), 1) >= HALF
    second = lax.broadcasted_iota(jnp.int32, (orders, LANES), 1) >= HALF
    columns, coeffs, ends, chosen, chosen_last = {}, {}, {}, {}, {}

    def arrange(tile):
        for pair in range(rows // 2):
            for odd in range(2):
                part = message_rows(wide, TILES * pair + (2 if tile == 2 else 3 * odd + tile), bands)[...]
                latitude(2 * pair + odd, tile)[...] = pltpu.roll(part, HALF, 1) if tile == 2 and odd else part
        columns[tile] = [
            grid[pl.ds(tile * orders + first, half), :].astype(BF16) for first in (own_first, other_first)
        ]

    def forward(j):
        own, other = columns[j // 2]
        if j in loads:
            loads[j].wait()
        table = own_table(j)
        coeffs[j] = dot(table[:orders, :], own, NN) + dot(other_ref[j, :orders, :], other, NN)
        ends[j] = dot(table[pl.ds(orders, 1), :], own, NN) + dot(other_ref[j, pl.ds(orders, 1), :], other, NN)

    def settle(tile):
        inside = [j for j in (2 * tile, 2 * tile + 1) if j < slots]
        both = coeffs[inside[0]] if len(inside) == 1 else jnp.where(second, coeffs[inside[1]], coeffs[inside[0]])
        turned = jnp.transpose(both)
        rest = jnp.zeros((8 - len(inside), LANES), F32)
        turned_ends = jnp.transpose(jnp.concatenate([ends[j] for j in inside] + [rest], axis=0))
        for n, j in enumerate(inside):
            mine = slice(n * four, (n + 1) * four)
            chosen[j] = (turned[mine] * gain_ref[j, :, pl.ds(0, orders)]).astype(BF16)
            chosen_last[j] = (turned_ends[mine, n : n + 1] * gain_ref[j, :, pl.ds(orders, 1)]).astype(BF16).astype(F32)

    def inverse(j):
        for table, first in ((own_table(j), own_first), (other_ref.at[j], other_first)):
            last = chosen_last[j] * table[pl.ds(orders, 1), :].astype(F32)
            back[pl.ds(j * four, four), pl.ds(first, half)] = dot(chosen[j], table[:orders, :], NN) + last

    def finish(tile):
        grid[pl.ds(tile * orders, orders), :] = jnp.transpose(back[pl.ds(tile * LANES, LANES), :])
        for pair in range(rows // 2):
            even, odd = latitude(2 * pair, tile)[...], latitude(2 * pair + 1, tile)[...]
            if tile == 2:
                both = jnp.where(right, pltpu.roll(odd, HALF, 1), even)
                message_rows(wide, TILES * pair + 2, bands)[...] = both
            else:
                message_rows(wide, TILES * pair + tile, bands)[...] = even
                message_rows(wide, TILES * pair + 3 + tile, bands)[...] = odd

    arrange(2)
    arrange(0)
    forward(4)
    forward(0)
    settle(2)
    inverse(4)
    forward(1)
    arrange(1)
    finish(2)
    forward(2)
    settle(0)
    inverse(0)
    forward(3)
    inverse(1)
    finish(0)
    settle(1)
    inverse(2)
    inverse(3)
    finish(1)
    message_rows(wide, ROWS - 1, bands)[...] = jnp.zeros((bands, LANES), F32)
    out_ref[...] = wide[...].astype(BF16)


def unpack_kernel(got_ref, points_ref, sel_ref, out_ref, wide, gathered, placed, held, out_sem):
    rows, _, levels, comps, orders = out_ref.shape
    bands = got_ref.shape[0] // ROWS
    vc = levels * comps
    group = 2 * vc
    per_tile = LANES // group
    wide[...] = got_ref[...].astype(F32)
    for pair in range(rows // 2):
        parts = [jnp.transpose(message_rows(wide, TILES * pair + u, bands)[...]).astype(BF16) for u in range(TILES)]
        for odd in range(2):
            tiles = [parts[3 * odd], parts[3 * odd + 1], parts[2][odd * HALF : (odd + 1) * HALF]]
            for n in range(2 * TILES):
                at = (n % per_tile) * group
                gathered[pl.ds((2 * pair + odd) * group, group), pl.ds(n * bands, bands)] = tiles[n // per_tile][
                    at : at + group
                ]
    column = lax.broadcasted_iota(jnp.int32, (comps, orders), 1)
    cut = rows // 2 * group
    stores = []
    for i in range(rows):
        if i in (0, rows // 2):
            lines = pl.ds(i * group, cut)
            placed[lines, :] = dot(gathered[lines, :], sel_ref[...], NN)
        live = (column <= cutoff_of(points_ref[i], orders)).astype(F32)
        for v in range(levels):
            even = placed[pl.ds(i * group + v * comps, comps), :]
            odd = placed[pl.ds(i * group + vc + v * comps, comps), :]
            held[i, 0, v] = ((even + odd) * live).astype(BF16)
            held[i, 1, v] = ((even - odd) * live).astype(BF16)
        stores.append(pltpu.make_async_copy(held.at[i], out_ref.at[i], out_sem.at[i]))
        stores[-1].start()
    for store in stores:
        store.wait()


def kernel_params(mib):
    return pltpu.CompilerParams(vmem_limit_bytes=mib * 1024 * 1024)


def exchange(packed, bands):
    shaped = packed.reshape(bands, ROWS // 2, 2, LANES)
    return lax.all_to_all(shaped, "band", split_axis=0, concat_axis=0, tiled=True).reshape(packed.shape)


def in_hbm(*arrays):
    return [pltpu.with_memory_space_constraint(a, pltpu.HBM) for a in arrays]


def in_vmem(*arrays):
    return [pltpu.with_memory_space_constraint(a, pltpu.VMEM) for a in arrays]


def on_device(bands, fourier_in, row_points, gauss_weight, pair_order, legendre, diffusion):
    rows, _, levels, comps, orders = fourier_in.shape
    slots, nrows, half = legendre.shape
    group = 2 * levels * comps
    size = (bands * ROWS, LANES)
    other = lax.ppermute(legendre, "lev", [(0, 1), (1, 0)])
    points, weights, order, kappas = in_hbm(row_points, gauss_weight, pair_order, diffusion.T)
    packed, selector, gain, early = pl.pallas_call(
        pack_kernel,
        out_shape=(
            pltpu.VMEM(size, BF16),
            pltpu.VMEM((orders, orders), BF16),
            pltpu.VMEM((slots, 2 * group, orders + LANES), F32),
            pltpu.VMEM((len(EARLY_SLOTS), nrows, half), BF16),
        ),
        in_specs=[ANY, ANY, ANY, ANY, ANY, VMEM, ANY],
        out_specs=(VMEM,) * 4,
        scratch_shapes=[
            pltpu.VMEM(fourier_in.shape, BF16),
            pltpu.SMEM(row_points.shape, jnp.int32),
            pltpu.SMEM(gauss_weight.shape, F32),
            pltpu.SMEM(pair_order.shape, jnp.int32),
            pltpu.SMEM(diffusion.shape[::-1], F32),
            pltpu.VMEM((group * rows, orders), F32),
            pltpu.VMEM(size, F32),
            pltpu.SemaphoreType.DMA((rows,)),
            pltpu.SemaphoreType.DMA((4,)),
            pltpu.SemaphoreType.DMA((len(EARLY_SLOTS),)),
        ],
        compiler_params=kernel_params(16),
        name="pack",
    )(*in_hbm(fourier_in), points, weights, order, kappas, order, *in_hbm(legendre))
    arrived = exchange(packed, bands)

    produced = pl.pallas_call(
        transform_kernel,
        out_shape=jax.ShapeDtypeStruct(size, BF16),
        in_specs=[VMEM, VMEM, ANY, VMEM, VMEM],
        out_specs=VMEM,
        scratch_shapes=[
            pltpu.VMEM((len(LATE_SLOTS), nrows, half), BF16),
            pltpu.VMEM(size, F32),
            pltpu.VMEM((3 * orders, LANES), F32),
            pltpu.VMEM((3 * LANES, orders), F32),
            pltpu.SemaphoreType.DMA((len(LATE_SLOTS),)),
        ],
        compiler_params=kernel_params(20),
        name="transform",
    )(arrived, *in_vmem(early), *in_hbm(legendre), *in_vmem(other, gain))
    landed = exchange(produced, bands)
    return pl.pallas_call(
        unpack_kernel,
        out_shape=jax.ShapeDtypeStruct(fourier_in.shape, BF16),
        in_specs=[VMEM, SMEM, VMEM],
        out_specs=ANY,
        scratch_shapes=[
            pltpu.VMEM(size, F32),
            pltpu.VMEM((group * rows, orders), BF16),
            pltpu.VMEM((group * rows, orders), F32),
            pltpu.VMEM(fourier_in.shape, BF16),
            pltpu.SemaphoreType.DMA((rows,)),
        ],
        compiler_params=kernel_params(16),
        name="unpack",
    )(landed, points, *in_vmem(selector))


def solution(mesh):
    in_specs = (
        P("band", None, "lev", None, None),
        P("band"),
        P("band"),
        P(),
        P("band", None, "lev"),
        P(),
    )
    out_specs = P("band", None, "lev", None, None)
    return jax.shard_map(
        functools.partial(on_device, mesh.shape["band"]),
        mesh=mesh,
        in_specs=in_specs,
        out_specs=out_specs,
        check_vma=False,
    )
```

```python
import functools

import jax
import jax.numpy as jnp
from jax import lax
from jax.experimental import pallas as pl
from jax.experimental.pallas import tpu as pltpu
from jax.sharding import PartitionSpec as P

F32 = jnp.float32
BF16 = jnp.bfloat16
LANES = 128
HALF = LANES // 2
NT = (((1,), (1,)), ((), ()))
NN = (((1,), (0,)), ((), ()))
VMEM = pl.BlockSpec(memory_space=pltpu.VMEM)
SMEM = pl.BlockSpec(memory_space=pltpu.SMEM)
ANY = pl.BlockSpec(memory_space=pl.ANY)
TILES = 5
ROWS = 26
EARLY_SLOTS = (4, 0)
LATE_SLOTS = (1, 2, 3)


def dot(a, b, dims):
    return lax.dot_general(a, b, dims, preferred_element_type=F32)


def one_hot_rows(listing, slot, q, orders, bands):
    slots = listing.shape[1] // bands
    where_ = lax.broadcasted_iota(jnp.int32, (bands, listing.shape[1]), 1)
    owner = lax.broadcasted_iota(jnp.int32, (bands, listing.shape[1]), 0)
    lead = jnp.sum(jnp.where(where_ == owner * slots + slot, listing, 0), axis=1, keepdims=True)
    order = lead if q == 0 else orders - 1 - lead
    column = lax.broadcasted_iota(jnp.int32, (bands, orders), 1)
    return jnp.where(column == order, 1.0, 0.0).astype(BF16)


def cutoff_of(points, orders):
    return jnp.minimum(orders - 1, lax.shift_right_arithmetic(points - 1, 1))


def message_rows(wide, row, bands):
    return wide.at[pl.ds(row, bands, stride=ROWS), :]


def one_hot(listing_ref, sel_ref):
    orders = sel_ref.shape[1]
    bands = orders // (2 * TILES)
    listing = listing_ref[...].reshape(1, orders // 2)
    for j in range(TILES):
        for q in range(2):
            sel_ref[pl.ds((2 * j + q) * bands, bands), :] = one_hot_rows(listing, j, q, orders, bands)


def pack_kernel(
    x_ref,
    points_in,
    weight_in,
    order_in,
    kappa_in,
    table_ref,
    out_ref,
    sel_ref,
    gain_ref,
    held_ref,
    x_held,
    points_ref,
    weight_ref,
    order_ref,
    kappa_ref,
    listing_ref,
    fold,
    wide,
    x_sem,
    own_sem,
    table_sem,
):
    rows, _, levels, comps, orders = x_ref.shape
    bands = sel_ref.shape[0] // (2 * TILES)
    vc = levels * comps
    group = 2 * vc
    column = lax.broadcasted_iota(jnp.int32, (comps, orders), 1)
    scalars = [
        (order_in, listing_ref),
        (order_in, order_ref),
        (kappa_in, kappa_ref),
        (points_in, points_ref),
        (weight_in, weight_ref),
    ]
    small = [pltpu.make_async_copy(a, b, own_sem.at[n]) for n, (a, b) in enumerate(scalars)]
    loads = [pltpu.make_async_copy(x_ref.at[i], x_held.at[i], x_sem.at[i]) for i in range(rows)]
    table = [
        pltpu.make_async_copy(table_ref.at[j], held_ref.at[n], table_sem.at[n]) for n, j in enumerate(EARLY_SLOTS)
    ]
    for load in small[:1] + loads + small[1:]:
        load.start()
    small[0].wait()
    one_hot(listing_ref, sel_ref)
    for load in small[1:]:
        load.wait()
    for load in table:
        load.start()
    damping(order_ref, kappa_ref, gain_ref)
    for i in range(rows):
        live = (column <= cutoff_of(points_ref[i], orders)).astype(F32)
        factor = live * weight_ref[i]
        loads[i].wait()
        for v in range(levels):
            north = x_held[i, 0, v].astype(F32)
            south = x_held[i, 1, v].astype(F32)
            fold[pl.ds(i * group + v * comps, comps), :] = (north + south) * factor
            fold[pl.ds(i * group + vc + v * comps, comps), :] = (north - south) * factor
    folded = fold[...].astype(BF16)
    per_tile = LANES // group
    for tile in range(3):
        first = tile * per_tile
        count = min(per_tile, 2 * TILES - first)
        sent = dot(folded, sel_ref[pl.ds(first * bands, count * bands), :], NT)

        def block(i):
            return [sent[i * group : (i + 1) * group, n * bands : (n + 1) * bands] for n in range(count)]

        for pair in range(rows // 2):
            if tile == 2:
                both = jnp.concatenate(block(2 * pair) + block(2 * pair + 1), axis=0)
                message_rows(wide, TILES * pair + 2, bands)[...] = jnp.transpose(both)
            else:
                for odd in range(2):
                    one = jnp.concatenate(block(2 * pair + odd), axis=0)
                    message_rows(wide, TILES * pair + 3 * odd + tile, bands)[...] = jnp.transpose(one)
    message_rows(wide, ROWS - 1, bands)[...] = jnp.zeros((bands, LANES), F32)
    out_ref[...] = wide[...].astype(BF16)
    for load in table:
        load.wait()


def damping(order_ref, kappa_ref, gain_ref):
    slots = gain_ref.shape[0]
    orders = gain_ref.shape[2] - LANES
    levels = kappa_ref.shape[1] // 2
    vc = 4 * levels
    band = lax.axis_index("band")
    lev = lax.axis_index("lev")
    which = lax.broadcasted_iota(jnp.int32, (vc, 1), 0)
    kappa = jnp.zeros((vc, 1), F32)
    for n in range(2 * levels):
        kappa = jnp.where(lax.shift_right_logical(which, 1) == n, kappa_ref[n % 2, lev * levels + n // 2], kappa)
    row = lax.broadcasted_iota(jnp.int32, (1, gain_ref.shape[2]), 1)
    odd = row > orders // 2
    odd_number = odd.astype(jnp.int32)
    position = row - odd_number * (orders // 2 + 1)
    for j in range(slots):
        first_order = order_ref[band * slots + j]
        second_order = orders - 1 - first_order
        boundary = jnp.where(
            odd,
            lax.shift_right_arithmetic(orders - first_order, 1),
            lax.shift_right_arithmetic(orders + 1 - first_order, 1),
        )
        leading = position < boundary
        degree = jnp.where(
            leading,
            first_order + odd_number + 2 * position,
            second_order + odd_number + 2 * (position - boundary),
        )
        growth = (degree * (degree + 1)).astype(F32) / float(orders * (orders + 1))
        factor = 1.0 / (1.0 + kappa * growth)
        for q in range(2):
            for p in range(2):
                mask = jnp.logical_and(
                    leading if q == 0 else jnp.logical_not(leading), odd if p == 1 else jnp.logical_not(odd)
                )
                gain_ref[j, pl.ds((2 * q + p) * vc, vc), :] = jnp.where(mask, factor, 0.0)


def transform_kernel(got_ref, early_ref, table_ref, other_ref, gain_ref, out_ref, late_ref, wide, grid, back, late_sem):
    slots, nrows, half = other_ref.shape
    orders = nrows - 1
    bands = got_ref.shape[0] // ROWS
    rows = orders // bands
    four = gain_ref.shape[1]
    lev = lax.axis_index("lev")
    own_first = pl.multiple_of(lev * half, LANES)
    other_first = pl.multiple_of((1 - lev) * half, LANES)

    loads = {
        j: pltpu.make_async_copy(table_ref.at[j], late_ref.at[n], late_sem.at[n]) for n, j in enumerate(LATE_SLOTS)
    }
    for load in loads.values():
        load.start()

    def own_table(j):
        return early_ref.at[EARLY_SLOTS.index(j)] if j in EARLY_SLOTS else late_ref.at[LATE_SLOTS.index(j)]

    def latitude(i, tile):
        return grid.at[pl.ds(tile * orders + i, bands, stride=rows), :]

    wide[...] = got_ref[...].astype(F32)
    right = lax.broadcasted_iota(jnp.int32, (bands, LANES), 1) >= HALF
    second = lax.broadcasted_iota(jnp.int32, (orders, LANES), 1) >= HALF
    columns, coeffs, ends, chosen, chosen_last = {}, {}, {}, {}, {}

    def arrange(tile):
        for pair in range(rows // 2):
            for odd in range(2):
                part = message_rows(wide, TILES * pair + (2 if tile == 2 else 3 * odd + tile), bands)[...]
                latitude(2 * pair + odd, tile)[...] = pltpu.roll(part, HALF, 1) if tile == 2 and odd else part
        columns[tile] = [
            grid[pl.ds(tile * orders + first, half), :].astype(BF16) for first in (own_first, other_first)
        ]

    def forward(j):
        own, other = columns[j // 2]
        if j in loads:
            loads[j].wait()
        table = own_table(j)
        coeffs[j] = dot(table[:orders, :], own, NN) + dot(other_ref[j, :orders, :], other, NN)
        ends[j] = dot(table[pl.ds(orders, 1), :], own, NN) + dot(other_ref[j, pl.ds(orders, 1), :], other, NN)

    def settle(tile):
        inside = [j for j in (2 * tile, 2 * tile + 1) if j < slots]
        both = coeffs[inside[0]] if len(inside) == 1 else jnp.where(second, coeffs[inside[1]], coeffs[inside[0]])
        turned = jnp.transpose(both)
        rest = jnp.zeros((8 - len(inside), LANES), F32)
        turned_ends = jnp.transpose(jnp.concatenate([ends[j] for j in inside] + [rest], axis=0))
        for n, j in enumerate(inside):
            mine = slice(n * four, (n + 1) * four)
            chosen[j] = (turned[mine] * gain_ref[j, :, pl.ds(0, orders)]).astype(BF16)
            chosen_last[j] = (turned_ends[mine, n : n + 1] * gain_ref[j, :, pl.ds(orders, 1)]).astype(BF16).astype(F32)

    def inverse(j):
        for table, first in ((own_table(j), own_first), (other_ref.at[j], other_first)):
            last = chosen_last[j] * table[pl.ds(orders, 1), :].astype(F32)
            back[pl.ds(j * four, four), pl.ds(first, half)] = dot(chosen[j], table[:orders, :], NN) + last

    def finish(tile):
        grid[pl.ds(tile * orders, orders), :] = jnp.transpose(back[pl.ds(tile * LANES, LANES), :])
        for pair in range(rows // 2):
            even, odd = latitude(2 * pair, tile)[...], latitude(2 * pair + 1, tile)[...]
            if tile == 2:
                both = jnp.where(right, pltpu.roll(odd, HALF, 1), even)
                message_rows(wide, TILES * pair + 2, bands)[...] = both
            else:
                message_rows(wide, TILES * pair + tile, bands)[...] = even
                message_rows(wide, TILES * pair + 3 + tile, bands)[...] = odd

    arrange(2)
    arrange(0)
    arrange(1)
    forward(4)
    forward(0)
    forward(1)
    forward(2)
    forward(3)
    settle(2)
    settle(0)
    settle(1)
    inverse(4)
    inverse(0)
    inverse(1)
    finish(2)
    finish(0)
    inverse(2)
    inverse(3)
    finish(1)
    message_rows(wide, ROWS - 1, bands)[...] = jnp.zeros((bands, LANES), F32)
    out_ref[...] = wide[...].astype(BF16)


def unpack_kernel(got_ref, points_in, sel_ref, out_ref, points_ref, wide, gathered, placed, held, points_sem, out_sem):
    points_load = pltpu.make_async_copy(points_in, points_ref, points_sem)
    points_load.start()
    rows, _, levels, comps, orders = out_ref.shape
    bands = got_ref.shape[0] // ROWS
    vc = levels * comps
    group = 2 * vc
    per_tile = LANES // group
    wide[...] = got_ref[...].astype(F32)
    for pair in range(rows // 2):
        parts = [jnp.transpose(message_rows(wide, TILES * pair + u, bands)[...]).astype(BF16) for u in range(TILES)]
        for odd in range(2):
            tiles = [parts[3 * odd], parts[3 * odd + 1], parts[2][odd * HALF : (odd + 1) * HALF]]
            for n in range(2 * TILES):
                at = (n % per_tile) * group
                gathered[pl.ds((2 * pair + odd) * group, group), pl.ds(n * bands, bands)] = tiles[n // per_tile][
                    at : at + group
                ]
    column = lax.broadcasted_iota(jnp.int32, (comps, orders), 1)
    cut = rows // 2 * group
    stores = []
    points_load.wait()
    for i in range(rows):
        if i in (0, rows // 2):
            lines = pl.ds(i * group, cut)
            placed[lines, :] = dot(gathered[lines, :], sel_ref[...], NN)
        live = (column <= cutoff_of(points_ref[i], orders)).astype(F32)
        for v in range(levels):
            even = placed[pl.ds(i * group + v * comps, comps), :]
            odd = placed[pl.ds(i * group + vc + v * comps, comps), :]
            held[i, 0, v] = ((even + odd) * live).astype(BF16)
            held[i, 1, v] = ((even - odd) * live).astype(BF16)
        stores.append(pltpu.make_async_copy(held.at[i], out_ref.at[i], out_sem.at[i]))
        stores[-1].start()
    for store in stores:
        store.wait()


def kernel_params(mib):
    return pltpu.CompilerParams(vmem_limit_bytes=mib * 1024 * 1024)


def exchange(packed, bands):
    shaped = packed.reshape(bands, ROWS // 2, 2, LANES)
    return lax.all_to_all(shaped, "band", split_axis=0, concat_axis=0, tiled=True).reshape(packed.shape)


def in_hbm(*arrays):
    return [pltpu.with_memory_space_constraint(a, pltpu.HBM) for a in arrays]


def in_vmem(*arrays):
    return [pltpu.with_memory_space_constraint(a, pltpu.VMEM) for a in arrays]


def on_device(bands, fourier_in, row_points, gauss_weight, pair_order, legendre, diffusion):
    rows, _, levels, comps, orders = fourier_in.shape
    slots, nrows, half = legendre.shape
    group = 2 * levels * comps
    size = (bands * ROWS, LANES)
    other = lax.ppermute(legendre, "lev", [(0, 1), (1, 0)])
    points, weights, order, kappas = in_hbm(row_points, gauss_weight, pair_order, diffusion.T)
    packed, selector, gain, early = pl.pallas_call(
        pack_kernel,
        out_shape=(
            pltpu.VMEM(size, BF16),
            pltpu.VMEM((orders, orders), BF16),
            pltpu.VMEM((slots, 2 * group, orders + LANES), F32),
            pltpu.VMEM((len(EARLY_SLOTS), nrows, half), BF16),
        ),
        in_specs=[ANY] * 6,
        out_specs=(VMEM,) * 4,
        scratch_shapes=[
            pltpu.VMEM(fourier_in.shape, BF16),
            pltpu.SMEM(row_points.shape, jnp.int32),
            pltpu.SMEM(gauss_weight.shape, F32),
            pltpu.SMEM(pair_order.shape, jnp.int32),
            pltpu.SMEM(diffusion.shape[::-1], F32),
            pltpu.VMEM(pair_order.shape, jnp.int32),
            pltpu.VMEM((group * rows, orders), F32),
            pltpu.VMEM(size, F32),
            pltpu.SemaphoreType.DMA((rows,)),
            pltpu.SemaphoreType.DMA((5,)),
            pltpu.SemaphoreType.DMA((len(EARLY_SLOTS),)),
        ],
        compiler_params=kernel_params(16),
        name="pack",
    )(*in_hbm(fourier_in), points, weights, order, kappas, *in_hbm(legendre))
    arrived = exchange(packed, bands)

    produced = pl.pallas_call(
        transform_kernel,
        out_shape=jax.ShapeDtypeStruct(size, BF16),
        in_specs=[VMEM, VMEM, ANY, VMEM, VMEM],
        out_specs=VMEM,
        scratch_shapes=[
            pltpu.VMEM((len(LATE_SLOTS), nrows, half), BF16),
            pltpu.VMEM(size, F32),
            pltpu.VMEM((3 * orders, LANES), F32),
            pltpu.VMEM((3 * LANES, orders), F32),
            pltpu.SemaphoreType.DMA((len(LATE_SLOTS),)),
        ],
        compiler_params=kernel_params(20),
        name="transform",
    )(arrived, *in_vmem(early), *in_hbm(legendre), *in_vmem(other, gain))
    landed = exchange(produced, bands)
    return pl.pallas_call(
        unpack_kernel,
        out_shape=jax.ShapeDtypeStruct(fourier_in.shape, BF16),
        in_specs=[VMEM, ANY, VMEM],
        out_specs=ANY,
        scratch_shapes=[
            pltpu.SMEM(row_points.shape, jnp.int32),
            pltpu.VMEM(size, F32),
            pltpu.VMEM((group * rows, orders), BF16),
            pltpu.VMEM((group * rows, orders), F32),
            pltpu.VMEM(fourier_in.shape, BF16),
            pltpu.SemaphoreType.DMA(()),
            pltpu.SemaphoreType.DMA((rows,)),
        ],
        compiler_params=kernel_params(16),
        name="unpack",
    )(landed, points, *in_vmem(selector))


def solution(mesh):
    in_specs = (
        P("band", None, "lev", None, None),
        P("band"),
        P("band"),
        P(),
        P("band", None, "lev"),
        P(),
    )
    out_specs = P("band", None, "lev", None, None)
    return jax.shard_map(
        functools.partial(on_device, mesh.shape["band"]),
        mesh=mesh,
        in_specs=in_specs,
        out_specs=out_specs,
        check_vma=False,
    )
```
